32 devices in a mesh: dp: 4 (over y, x), expert: 8 (over z, core).
Axes of the slice: x: 2, y: 2, z: 4, core: 2. Of those that a mesh axis runs over, the one named last changes fastest.
Arguments:
- tokens: bfloat16 [4096, 2048], P(('dp', 'expert')), may hold values from -6 to 6
- cotangent: bfloat16 [4096, 2048], P(('dp', 'expert')), may hold values from -6 to 6
- expert_ids: int32 [4096, 6], P(('dp', 'expert')), may hold values from 0 to 7, as said below
- gate_fixed: int32 [4096, 6], P(('dp', 'expert')), may hold values from 1024 to 65535
- w_gate: bfloat16 [8, 2048, 704], P('expert'), may hold values from -0.125 to 0.125
- w_up: bfloat16 [8, 2048, 704], P('expert'), may hold values from -0.125 to 0.125
- w_down: bfloat16 [8, 704, 2048], P('expert'), may hold values from -0.21875 to 0.21875
Outputs:
- mixed: bfloat16 [4096, 2048], P(('dp', 'expert'))
- token_grad: bfloat16 [4096, 2048], P(('dp', 'expert'))
- grad_gate: float32 [8, 2048, 704], P('expert', 'dp')
- grad_up: float32 [8, 2048, 704], P('expert', 'dp')
- grad_down: float32 [8, 704, 2048], P('expert', None, 'dp')
The draws below stay inside these ranges and needn't reach their ends.
Inputs may be any that keep to these rules, and one draw needn't show every extreme that they name: `expert_ids`: each row names 6 different experts. Within the rows of one device (aligned blocks of 128 rows) no expert is named by more than 128 rows, and one expert, the same in every block, is named by exactly 128 rows.
All inputs are finite; a program needn't handle non-finite values.
Results may differ from the reference program's by a relative error of at most 0.0095.
Values may be sent and summed in bfloat16 or wider, within the bound.
No kernel may reach another device: no remote copies, remote signals or barrier semaphores. Data moves between devices by JAX's collectives and lax.ppermute only.
A program may use at most 192 MiB of HBM per device.

```python
import jax
import jax.numpy as jnp
from jax import lax

D = 2048
FF = 704
TOP = 6
TOK_DEV = 128
EXPERTS = 8
CAP = 128
TOKENS = 4096
N_DP = 4
N_EXPERT = 8


def draw_expert_ids(key, part):
    block_count = TOKENS // TOK_DEV
    slot_total = TOK_DEV * TOP
    full_expert = jax.random.randint(jax.random.fold_in(key, 11), (), 0, EXPERTS)
    others = EXPERTS - 1
    rest_slots = slot_total - CAP
    base_load = rest_slots // others
    extra_count = rest_slots % others
    pair_count = others // 2

    def one_block(block_key):
        key_a, key_b, key_c, key_d = jax.random.split(block_key, 4)
        loads = base_load + (jnp.arange(others) < extra_count).astype(jnp.int32)
        loads = jax.random.permutation(key_a, loads)
        giver_load = loads[0:2 * pair_count:2]
        taker_load = loads[1:2 * pair_count:2]
        room_left = jnp.minimum(giver_load - 1, CAP - taker_load)
        moved_rows = jax.random.randint(key_b, (pair_count,), 0, room_left + 1)
        loads = loads.at[0:2 * pair_count:2].add(-moved_rows)
        loads = loads.at[1:2 * pair_count:2].add(moved_rows)
        expert_index = jnp.arange(EXPERTS)
        other_pos = jnp.clip(expert_index - (expert_index > full_expert).astype(jnp.int32), 0, others - 1)
        counts = jnp.where(expert_index == full_expert, CAP, loads[other_pos])
        run_order = jax.random.permutation(key_c, EXPERTS)
        run_ends = jnp.cumsum(counts[run_order])
        labels = run_order[jnp.sum((run_ends[None, :] <= jnp.arange(slot_total)[:, None]).astype(jnp.int32), axis=1)]
        table_rows = labels.reshape(TOP, TOK_DEV).T
        return table_rows[jax.random.permutation(key_d, TOK_DEV)]
    block_keys = jax.random.split(jax.random.fold_in(key, 23), block_count)
    return jax.vmap(one_block)(block_keys).reshape(TOKENS, TOP).astype(jnp.int32)


def plant(result, stream_key, low, top_value):
    spot = [jax.random.randint(jax.random.fold_in(stream_key, axis), (), 0, length) for axis, length in enumerate(result.shape)]
    main_axis = result.shape.index(max(result.shape))
    beside = spot[:main_axis] + [(spot[main_axis] + 1) % result.shape[main_axis]] + spot[main_axis + 1:]
    return result.at[tuple(spot)].set(low).at[tuple(beside)].set(top_value)


def levels(rng, shape, cuts, least, top_value):
    def one(dim, parts):
        heights = jax.random.uniform(jax.random.fold_in(jax.random.fold_in(rng, 6), dim), (parts,), jnp.float32, least / len(cuts), top_value / len(cuts))
        return jnp.repeat(jnp.exp(heights), shape[dim] // parts).reshape((-1,) + (1,) * (len(shape) - dim - 1))

    gain = one(*cuts[0])
    for cut in cuts[1:]:
        gain = gain * one(*cut)
    return gain


def centred(key, shape, width, limit, cuts=(), held_as=jnp.bfloat16):
    drawn = width * jax.random.normal(key, shape, jnp.float32)
    if cuts:
        drawn = drawn * levels(key, shape, cuts, -0.22, 0.18)
    return jnp.clip(drawn, -limit, limit).astype(held_as)


def setup_inputs(seed: int = 0) -> dict:
    streams_of = jax.random.split(jax.random.key(seed), 8)
    tokens = centred(streams_of[0], (TOKENS, D), 1.0, 6.0, ((0, 32),))
    cotangent = centred(streams_of[1], (TOKENS, D), 1.0, 6.0, ((0, 32),))
    expert_ids = draw_expert_ids(jax.random.fold_in(streams_of[7], 71), 0)
    gate_fixed = plant(jax.random.randint(streams_of[3], (TOKENS, TOP), 1024, 65536), jax.random.fold_in(streams_of[3], 1), 1024, 65535).astype(jnp.int32)
    w_gate = centred(streams_of[4], (EXPERTS, D, FF), D ** -0.5, 0.125, ((0, 8),))
    w_up = centred(streams_of[5], (EXPERTS, D, FF), D ** -0.5, 0.125, ((0, 8),))
    w_down = centred(streams_of[6], (EXPERTS, FF, D), FF ** -0.5, 0.21875, ((0, 8),))
    return {"tokens": tokens, "cotangent": cotangent, "expert_ids": expert_ids, "gate_fixed": gate_fixed, "w_gate": w_gate, "w_up": w_up, "w_down": w_down}


def reference(tokens, cotangent, expert_ids, gate_fixed, w_gate, w_up, w_down):
    flat_ids = expert_ids.reshape(-1)
    gate_values = gate_fixed.reshape(-1).astype(jnp.float32) / 65536.0
    max_rows = N_DP * N_EXPERT * CAP
    pair_total = TOKENS * TOP

    def per_expert(carry, expert_no):
        out_acc, grad_acc = carry
        matches = flat_ids == expert_no
        picked = jnp.nonzero(matches, size=max_rows, fill_value=pair_total)[0].astype(jnp.int32)
        is_valid = picked < pair_total
        safe_pick = jnp.where(is_valid, picked, 0).astype(jnp.int32)
        token_row = (safe_pick // TOP).astype(jnp.int32)
        rows_in = jnp.where(is_valid[:, None], tokens[token_row], jnp.zeros((), tokens.dtype))
        gate_rows = jnp.where(is_valid, gate_values[safe_pick], jnp.zeros((), jnp.float32))
        gate_w = w_gate[expert_no]
        up_w = w_up[expert_no]
        down_w = w_down[expert_no]
        gate_pre = jnp.dot(rows_in, gate_w, preferred_element_type=jnp.float32)
        up_pre = jnp.dot(rows_in, up_w, preferred_element_type=jnp.float32)
        sigma = jax.nn.sigmoid(gate_pre)
        activ = gate_pre * sigma
        hidden = (activ * up_pre).astype(jnp.bfloat16)
        expert_out = jnp.dot(hidden, down_w, preferred_element_type=jnp.float32).astype(jnp.bfloat16)
        dy_pair = (cotangent[token_row].astype(jnp.float32) * gate_rows[:, None]).astype(jnp.bfloat16)
        d_hidden = jnp.dot(dy_pair, down_w.T, preferred_element_type=jnp.float32)
        d_gate = (d_hidden * up_pre * (sigma * (1.0 + gate_pre * (1.0 - sigma)))).astype(jnp.bfloat16)
        d_up = (d_hidden * activ).astype(jnp.bfloat16)
        d_rows = (jnp.dot(d_gate, gate_w.T, preferred_element_type=jnp.float32)
                  + jnp.dot(d_up, up_w.T, preferred_element_type=jnp.float32)).astype(jnp.bfloat16)
        target = jnp.where(is_valid, token_row, TOKENS).astype(jnp.int32)
        out_acc = out_acc.at[target].add(gate_rows[:, None] * expert_out.astype(jnp.float32), mode="drop")
        grad_acc = grad_acc.at[target].add(d_rows.astype(jnp.float32), mode="drop")
        grad_gate = jnp.dot(rows_in.T, d_gate, preferred_element_type=jnp.float32)
        grad_up = jnp.dot(rows_in.T, d_up, preferred_element_type=jnp.float32)
        grad_down = jnp.dot(hidden.T, dy_pair, preferred_element_type=jnp.float32)
        return (out_acc, grad_acc), (grad_gate, grad_up, grad_down)

    start_carry = (jnp.zeros((TOKENS, D), jnp.float32), jnp.zeros((TOKENS, D), jnp.float32))
    (out_acc, grad_acc), (grad_gate, grad_up, grad_down) = lax.scan(
        per_expert, start_carry, jnp.arange(EXPERTS, dtype=jnp.int32))
    return (out_acc.astype(jnp.bfloat16), grad_acc.astype(jnp.bfloat16), grad_gate, grad_up, grad_down)
```

```python
from functools import partial

import jax
import jax.numpy as jnp
from jax import lax
from jax.sharding import PartitionSpec as P


def contract(left, right):
    return lax.dot_general(
        left, right, (((0,), (0,)), ((), ())), preferred_element_type=jnp.float32
    )


def trans_dot(left, right):
    return lax.dot_general(
        left, right, (((1,), (1,)), ((), ())), preferred_element_type=jnp.float32
    )


def forward_rows(gate_w, up_w, down_w, rows_in):
    gate_pre = jnp.dot(rows_in, gate_w, preferred_element_type=jnp.float32)
    up_pre = jnp.dot(rows_in, up_w, preferred_element_type=jnp.float32)
    hidden = (gate_pre * jax.nn.sigmoid(gate_pre) * up_pre).astype(jnp.bfloat16)
    expert_out = jnp.dot(hidden, down_w, preferred_element_type=jnp.float32).astype(jnp.bfloat16)
    return (expert_out, gate_pre, up_pre, hidden)


def backward_rows(gate_w, up_w, down_w, dy_rows, gate_pre, up_pre):
    sigma = jax.nn.sigmoid(gate_pre)
    activ = gate_pre * sigma
    d_hidden = trans_dot(dy_rows, down_w)
    d_gate = (d_hidden * up_pre * (sigma * (1.0 + gate_pre * (1.0 - sigma)))).astype(jnp.bfloat16)
    d_up = (d_hidden * activ).astype(jnp.bfloat16)
    d_rows = (trans_dot(d_gate, gate_w) + trans_dot(d_up, up_w)).astype(jnp.bfloat16)
    return (d_rows, d_gate, d_up)


def slot_shards(tokens, cotangent, expert_ids, gate_fixed, w_gate, w_up, w_down):
    n_expert = lax.axis_size("expert")
    tok_rows = tokens.shape[0]
    width = tokens.shape[1]
    top_k = expert_ids.shape[1]
    capacity = 4 * tok_rows * top_k // (3 * n_expert)
    slot_count = n_expert * capacity
    gate_w = w_gate[0]
    up_w = w_up[0]
    down_w = w_down[0]
    flat_ids = expert_ids.reshape(-1)
    onehot = (flat_ids[:, None] == jnp.arange(n_expert, dtype=jnp.int32)[None, :]).astype(jnp.int32)
    before = jnp.cumsum(onehot, axis=0) - onehot
    rank_in = jnp.sum(before * onehot, axis=1)
    counts = jnp.sum(onehot, axis=0)
    slot_of = flat_ids * capacity + rank_in
    owner = jnp.arange(flat_ids.shape[0], dtype=jnp.int32) // top_k
    slot_token = jnp.zeros((slot_count,), jnp.int32).at[slot_of].set(owner)
    gate_values = gate_fixed.reshape(-1).astype(jnp.float32) / 65536.0
    slot_gate = jnp.zeros((slot_count,), jnp.float32).at[slot_of].set(gate_values)
    outgoing = jnp.where(
        (slot_gate > 0.0)[:, None], tokens[slot_token], jnp.zeros((), tokens.dtype)
    )
    received, arrived = (
        lax.all_to_all(outgoing, "expert", split_axis=0, concat_axis=0, tiled=True),
        lax.all_to_all(counts, "expert", split_axis=0, concat_axis=0, tiled=True),
    )

    def run_rows(row_fn, inputs):
        return row_fn(*inputs)

    def fold_rows(left, right):
        return contract(left, right)

    expert_out, gate_pre, up_pre, hidden = run_rows(
        partial(forward_rows, gate_w, up_w, down_w), (received,)
    )
    returned = lax.all_to_all(expert_out, "expert", split_axis=0, concat_axis=0, tiled=True)
    mixed_rows = returned[slot_of].astype(jnp.float32).reshape(tok_rows, top_k, width)
    mixed = jnp.sum(mixed_rows * gate_values.reshape(tok_rows, top_k)[:, :, None], axis=1).astype(
        jnp.bfloat16
    )
    dy_out = (cotangent[slot_token].astype(jnp.float32) * slot_gate[:, None]).astype(jnp.bfloat16)
    dy_in = lax.all_to_all(dy_out, "expert", split_axis=0, concat_axis=0, tiled=True)
    d_rows, d_gate, d_up = run_rows(
        partial(backward_rows, gate_w, up_w, down_w), (dy_in, gate_pre, up_pre)
    )
    back_rows = lax.all_to_all(d_rows, "expert", split_axis=0, concat_axis=0, tiled=True)
    token_grad = jnp.sum(
        back_rows[slot_of].astype(jnp.float32).reshape(tok_rows, top_k, width), axis=1
    ).astype(jnp.bfloat16)
    grad_gate, grad_up, grad_down = (
        lax.psum_scatter(
            fold_rows(received, d_gate).astype(jnp.bfloat16), "dp", scatter_dimension=0, tiled=True
        ).astype(jnp.float32),
        lax.psum_scatter(
            fold_rows(received, d_up).astype(jnp.bfloat16), "dp", scatter_dimension=0, tiled=True
        ).astype(jnp.float32),
        lax.psum_scatter(
            fold_rows(hidden, dy_in).astype(jnp.bfloat16), "dp", scatter_dimension=1, tiled=True
        ).astype(jnp.float32),
    )
    return (mixed, token_grad, grad_gate[None], grad_up[None], grad_down[None])


def ring_order(count):
    return [0] + list(range(1, count, 2)) + [at for at in range(count - 1, 1, -1) if at % 2 == 0]


def ring_pairs(n_expert):
    order = ring_order(n_expert // 2)
    follow = {at: order[(spot + 1) % len(order)] for spot, at in enumerate(order)}
    return [(2 * at + core, 2 * follow[at] + core) for at in order for core in range(2)]


def pair_pairs(n_expert):
    return [(at, at ^ 1) for at in range(n_expert)]


def gather_rows(mine, n_expert):
    shards_in = [mine]
    for _ in range(n_expert // 2 - 1):
        shards_in.append(lax.ppermute(shards_in[-1], "expert", ring_pairs(n_expert)))
    out = []
    for shard in shards_in:
        out.append((shard, lax.ppermute(shard, "expert", pair_pairs(n_expert))))
    return out


def add_rows(left, right):
    return left.astype(jnp.float32) + right.astype(jnp.float32)


def scatter_rows(partials, n_expert):
    kept = []
    for mine, other in partials:
        arrived = lax.ppermute(other, "expert", pair_pairs(n_expert))
        kept.append(add_rows(mine, arrived))
    steps = len(kept)
    moving = kept[1 % steps]
    for step in range(1, steps):
        moving = lax.ppermute(moving.astype(jnp.bfloat16), "expert", ring_pairs(n_expert))
        moving = add_rows(moving, kept[(step + 1) % steps])
    return moving.astype(jnp.bfloat16)


def reduce_dp(grads, n_dp, dim):
    size = grads.shape[dim] // n_dp
    me = lax.axis_index("dp")
    pairs = [[(at, at ^ flip) for at in range(n_dp)] for flip in (1, 2)]

    def block(owner, half):
        return lax.dynamic_slice_in_dim(grads, owner * size + half * (size // 2), size // 2, dim)

    out = []
    for half, (first, second) in enumerate(((1, 2), (2, 1))):
        sent = [lax.ppermute(block(me ^ first ^ far, half), "dp", pairs[first - 1]) for far in (second, 0)]
        far_sum = add_rows(block(me ^ second, half), sent[0]).astype(jnp.bfloat16)
        near_sum = add_rows(block(me, half), sent[1])
        out.append(add_rows(near_sum, lax.ppermute(far_sum, "dp", pairs[second - 1])))
    return jnp.concatenate(out, axis=dim)


def dense_shards(tokens, cotangent, expert_ids, gate_fixed, w_gate, w_up, w_down):
    n_expert = lax.axis_size("expert")
    n_dp = lax.axis_size("dp")
    expert = lax.axis_index("expert")
    gate_w, up_w, down_w = w_gate[0], w_up[0], w_down[0]
    gate_values = gate_fixed.astype(jnp.float32) / 65536.0
    table = jnp.sum(
        jnp.where(
            expert_ids[:, :, None] == jnp.arange(n_expert, dtype=jnp.int32)[None, None, :],
            gate_values[:, :, None],
            0.0,
        ),
        axis=1,
    )
    tables = gather_rows(table, n_expert)
    token_rows = gather_rows(tokens, n_expert)
    cot_rows = gather_rows(cotangent, n_expert)

    def flat(parts):
        return jnp.concatenate([part for pair in parts for part in pair], axis=0)

    rows = flat(token_rows)
    cots = flat(cot_rows)
    all_tables = flat(tables)
    weight = jnp.sum(
        jnp.where(jnp.arange(n_expert, dtype=jnp.int32)[None, :] == expert, all_tables, 0.0), axis=1, keepdims=True
    )

    def unflat(partial):
        parts = jnp.split(partial, n_expert, axis=0)
        return list(zip(parts[0::2], parts[1::2]))

    gate_pre = jnp.dot(rows, gate_w, preferred_element_type=jnp.float32)
    up_pre = jnp.dot(rows, up_w, preferred_element_type=jnp.float32)
    hidden = (gate_pre * jax.nn.sigmoid(gate_pre) * up_pre).astype(jnp.bfloat16)
    expert_out = jnp.dot(hidden, down_w, preferred_element_type=jnp.float32)
    mixed = scatter_rows(unflat((expert_out * weight).astype(jnp.bfloat16)), n_expert)
    dy_rows = (cots.astype(jnp.float32) * weight).astype(jnp.bfloat16)
    grad_down = reduce_dp(contract(hidden, dy_rows).astype(jnp.bfloat16), n_dp, 1)
    d_rows, d_gate, d_up = backward_rows(gate_w, up_w, down_w, dy_rows, gate_pre, up_pre)
    grad_gate = reduce_dp(contract(rows, d_gate).astype(jnp.bfloat16), n_dp, 0)
    grad_up = reduce_dp(contract(rows, d_up).astype(jnp.bfloat16), n_dp, 0)
    token_grad = scatter_rows(unflat(d_rows), n_expert)
    return (mixed, token_grad, grad_gate[None], grad_up[None], grad_down[None])


def shards(tokens, cotangent, expert_ids, gate_fixed, w_gate, w_up, w_down):
    n_expert = lax.axis_size("expert")
    capacity = 4 * tokens.shape[0] * expert_ids.shape[1] // (3 * n_expert)
    dense = capacity >= tokens.shape[0] and n_expert % 2 == 0 and lax.axis_size("dp") == 4
    run = dense_shards if dense else slot_shards
    return run(tokens, cotangent, expert_ids, gate_fixed, w_gate, w_up, w_down)


def solution(mesh):
    in_specs = (
        P(("dp", "expert"), None),
        P(("dp", "expert"), None),
        P(("dp", "expert"), None),
        P(("dp", "expert"), None),
        P("expert", None, None),
        P("expert", None, None),
        P("expert", None, None),
    )
    out_specs = (
        P(("dp", "expert"), None),
        P(("dp", "expert"), None),
        P("expert", "dp", None),
        P("expert", "dp", None),
        P("expert", None, "dp"),
    )
    return jax.shard_map(shards, mesh=mesh, in_specs=in_specs, out_specs=out_specs, check_vma=False)
```

```python
from functools import partial

import jax
import jax.numpy as jnp
from jax import lax
from jax.experimental import pallas as pl
from jax.experimental.pallas import tpu as pltpu
from jax.sharding import PartitionSpec as P


def contract(left, right):
    return lax.dot_general(
        left, right, (((0,), (0,)), ((), ())), preferred_element_type=jnp.float32
    )


def trans_dot(left, right):
    return lax.dot_general(
        left, right, (((1,), (1,)), ((), ())), preferred_element_type=jnp.float32
    )


def forward_rows(gate_w, up_w, down_w, rows_in):
    gate_pre = jnp.dot(rows_in, gate_w, preferred_element_type=jnp.float32)
    up_pre = jnp.dot(rows_in, up_w, preferred_element_type=jnp.float32)
    hidden = (gate_pre * jax.nn.sigmoid(gate_pre) * up_pre).astype(jnp.bfloat16)
    expert_out = jnp.dot(hidden, down_w, preferred_element_type=jnp.float32).astype(jnp.bfloat16)
    return (expert_out, gate_pre, up_pre, hidden)


def backward_rows(gate_w, up_w, down_w, dy_rows, gate_pre, up_pre):
    sigma = jax.nn.sigmoid(gate_pre)
    activ = gate_pre * sigma
    d_hidden = trans_dot(dy_rows, down_w)
    d_gate = (d_hidden * up_pre * (sigma * (1.0 + gate_pre * (1.0 - sigma)))).astype(jnp.bfloat16)
    d_up = (d_hidden * activ).astype(jnp.bfloat16)
    d_rows = (trans_dot(d_gate, gate_w) + trans_dot(d_up, up_w)).astype(jnp.bfloat16)
    return (d_rows, d_gate, d_up)


def slot_shards(tokens, cotangent, expert_ids, gate_fixed, w_gate, w_up, w_down):
    n_expert = lax.axis_size("expert")
    tok_rows = tokens.shape[0]
    width = tokens.shape[1]
    top_k = expert_ids.shape[1]
    capacity = 4 * tok_rows * top_k // (3 * n_expert)
    slot_count = n_expert * capacity
    gate_w = w_gate[0]
    up_w = w_up[0]
    down_w = w_down[0]
    flat_ids = expert_ids.reshape(-1)
    onehot = (flat_ids[:, None] == jnp.arange(n_expert, dtype=jnp.int32)[None, :]).astype(jnp.int32)
    before = jnp.cumsum(onehot, axis=0) - onehot
    rank_in = jnp.sum(before * onehot, axis=1)
    counts = jnp.sum(onehot, axis=0)
    slot_of = flat_ids * capacity + rank_in
    owner = jnp.arange(flat_ids.shape[0], dtype=jnp.int32) // top_k
    slot_token = jnp.zeros((slot_count,), jnp.int32).at[slot_of].set(owner)
    gate_values = gate_fixed.reshape(-1).astype(jnp.float32) / 65536.0
    slot_gate = jnp.zeros((slot_count,), jnp.float32).at[slot_of].set(gate_values)
    outgoing = jnp.where(
        (slot_gate > 0.0)[:, None], tokens[slot_token], jnp.zeros((), tokens.dtype)
    )
    received, arrived = (
        lax.all_to_all(outgoing, "expert", split_axis=0, concat_axis=0, tiled=True),
        lax.all_to_all(counts, "expert", split_axis=0, concat_axis=0, tiled=True),
    )

    def run_rows(row_fn, inputs):
        return row_fn(*inputs)

    def fold_rows(left, right):
        return contract(left, right)

    expert_out, gate_pre, up_pre, hidden = run_rows(
        partial(forward_rows, gate_w, up_w, down_w), (received,)
    )
    returned = lax.all_to_all(expert_out, "expert", split_axis=0, concat_axis=0, tiled=True)
    mixed_rows = returned[slot_of].astype(jnp.float32).reshape(tok_rows, top_k, width)
    mixed = jnp.sum(mixed_rows * gate_values.reshape(tok_rows, top_k)[:, :, None], axis=1).astype(
        jnp.bfloat16
    )
    dy_out = (cotangent[slot_token].astype(jnp.float32) * slot_gate[:, None]).astype(jnp.bfloat16)
    dy_in = lax.all_to_all(dy_out, "expert", split_axis=0, concat_axis=0, tiled=True)
    d_rows, d_gate, d_up = run_rows(
        partial(backward_rows, gate_w, up_w, down_w), (dy_in, gate_pre, up_pre)
    )
    back_rows = lax.all_to_all(d_rows, "expert", split_axis=0, concat_axis=0, tiled=True)
    token_grad = jnp.sum(
        back_rows[slot_of].astype(jnp.float32).reshape(tok_rows, top_k, width), axis=1
    ).astype(jnp.bfloat16)
    grad_gate, grad_up, grad_down = (
        lax.psum_scatter(
            fold_rows(received, d_gate).astype(jnp.bfloat16), "dp", scatter_dimension=0, tiled=True
        ).astype(jnp.float32),
        lax.psum_scatter(
            fold_rows(received, d_up).astype(jnp.bfloat16), "dp", scatter_dimension=0, tiled=True
        ).astype(jnp.float32),
        lax.psum_scatter(
            fold_rows(hidden, dy_in).astype(jnp.bfloat16), "dp", scatter_dimension=1, tiled=True
        ).astype(jnp.float32),
    )
    return (mixed, token_grad, grad_gate[None], grad_up[None], grad_down[None])


BF16, F32 = jnp.bfloat16, jnp.float32
VMEM = pl.BlockSpec(memory_space=pltpu.VMEM)
SMEM = pl.BlockSpec(memory_space=pltpu.SMEM)
PIECES = ((1, 0), (3, 0), (2, 1), (3, 1), (0, 0), (2, 0), (0, 1), (1, 1))


def tie(*values):
    return lax.optimization_barrier(values)


def nt(left, right):
    return lax.dot_general(left, right, (((1,), (1,)), ((), ())), preferred_element_type=F32)


def nn(left, right):
    return lax.dot_general(left, right, (((1,), (0,)), ((), ())), preferred_element_type=F32)


def tn(left, right):
    return lax.dot_general(left, right, (((0,), (0,)), ((), ())), preferred_element_type=F32)


def call(name, kernel, outs, ins, scratch=(), smem=0):
    return list(pl.pallas_call(
        kernel,
        name=name,
        out_shape=[jax.ShapeDtypeStruct(shape, dtype) for shape, dtype in outs],
        in_specs=[SMEM] * smem + [VMEM] * (len(ins) - smem),
        out_specs=[VMEM] * len(outs),
        scratch_shapes=[pltpu.VMEM(shape, dtype) for shape, dtype in scratch],
        compiler_params=pltpu.CompilerParams(vmem_limit_bytes=16 * 1024 * 1024),
        cost_estimate=pl.CostEstimate(flops=1, bytes_accessed=1, transcendentals=0),
    )(*ins))


def per_row(weights, row, width):
    count = weights.shape[1]
    square = jnp.broadcast_to(weights[row : row + 1, :], (count, count)).T
    return jnp.concatenate([square] * (width // count), axis=1)


def split_kernel(offs, whole, part_s, part_k):
    size = whole.shape[1] // 8
    for at in range(8):
        here = pl.ds(pl.multiple_of(offs[at], size), size)
        (part_s if at < 4 else part_k)[:, pl.ds(at % 4 * size, size)] = whole[:, here]


def forward_kernel(
    slot, offs, weights, mine_a, mine_b, other_a, other_b, gate, up, down, hid, fac_g, fac_u, out_m, out_o, rows_s, rows_k, rows
):
    n, width = out_m.shape
    size = width // 8
    stack((mine_a, mine_b, other_a, other_b), rows)
    gate_pre = nt(rows[...], gate[...])
    up_pre = nt(rows[...], up[...])
    sigma = jax.nn.sigmoid(gate_pre)
    activ = gate_pre * sigma
    hidden = (activ * up_pre).astype(BF16)
    hid[...] = hidden
    fac_g[...] = up_pre * (sigma * (1.0 + gate_pre * (1.0 - sigma)))
    fac_u[...] = activ
    out = nn(hidden, down[...])
    out_m[...] = (out[:n] * per_row(weights[...], slot, width)).astype(BF16)
    out_o[...] = (out[n:] * per_row(weights[...], slot + 4, width)).astype(BF16)
    for at in range(8):
        here = pl.ds(pl.multiple_of(offs[at], size), size)
        (rows_s if at < 4 else rows_k)[:, pl.ds(at % 4 * size, size)] = rows[:, here]


def fill_dy(weights, cots, dy):
    n, width = cots[0].shape
    for slot in range(4):
        for core in range(2):
            row = slot + 4 * core
            at = (2 * slot + core) * n
            dy[at : at + n, :] = (cots[row][...].astype(F32) * per_row(weights[...], row, width)).astype(BF16)


def early_kernel(weights, *refs):
    cots, hids, (down, sent_a, sent_b, d_hid, dy, hid) = refs[:8], refs[8:12], refs[12:]
    n = hids[0].shape[0]
    fill_dy(weights, cots, dy)
    for slot in range(4):
        hid[slot * n : (slot + 1) * n, :] = hids[slot][...]
    half = dy.shape[1] // 2
    sent_a[...] = tn(hid[...], dy[:, :half]).astype(BF16)
    sent_b[...] = tn(hid[...], dy[:, half:]).astype(BF16)
    for at in range(2):
        part = pl.ds(at * 2 * n, 2 * n)
        d_hid[part, :] = nt(dy[part, :], down[...])


def late_kernel(weights, *refs):
    cots, facs_g, facs_u, (d_early, down, d_gate, d_up, dy) = refs[:8], refs[8:12], refs[12:16], refs[16:]
    n = facs_g[0].shape[0]
    fill_dy(weights, cots, dy)
    for slot in range(4):
        part = pl.ds(slot * n, n)
        d_hid = d_early[part, :] + nt(dy[part, :], down[...])
        d_gate[part, :] = (d_hid * facs_g[slot][...]).astype(BF16)
        d_up[part, :] = (d_hid * facs_u[slot][...]).astype(BF16)


def stack(parts, whole):
    n = parts[0].shape[0]
    for at, part in enumerate(parts):
        whole[at * n : (at + 1) * n, :] = part[...]


def grads_kernel(left, *refs):
    rights, (out_a, out_b, right) = refs[:-3], refs[-3:]
    stack(rights, right)
    half = right.shape[1] // 2
    out_a[...] = tn(left[...], right[:, :half]).astype(BF16)
    out_b[...] = tn(left[...], right[:, half:]).astype(BF16)


def hidden_grads_kernel(right, *refs):
    hids, (out_a, out_b, left) = refs[:4], refs[4:]
    stack(hids, left)
    half = right.shape[1] // 2
    out_a[...] = tn(left[...], right[:, :half]).astype(BF16)
    out_b[...] = tn(left[...], right[:, half:]).astype(BF16)


def cross_kernel(count, *refs):
    ins, (far_a, far_b, near_a, near_b) = refs[: 4 * count], refs[4 * count :]
    cut = far_a.shape[2]
    for at in range(count):
        came_a, came_b, own_a, own_b = ins[4 * at : 4 * at + 4]
        for came, own, far, near in ((came_a, own_a, far_a, near_a), (came_b, own_b, far_b, near_b)):
            both = came[...].astype(F32) + own[...].astype(F32)
            near[at, :, :] = both[:, :cut]
            far[at, :, :] = both[:, cut:].astype(BF16)


def rows_kernel(slots, d_gate, d_up, gate, up, mine, other):
    n = mine.shape[0] // len(slots)
    for at, slot in enumerate(slots):
        part = pl.ds(slot * 2 * n, 2 * n)
        both = nn(d_gate[part, :], gate[...]) + nn(d_up[part, :], up[...])
        mine[at * n : (at + 1) * n, :] = both[:n].astype(BF16)
        other[at * n : (at + 1) * n, :] = both[n:].astype(BF16)


def ring_order(count):
    return [0] + list(range(1, count, 2)) + [at for at in range(count - 1, 1, -1) if at % 2 == 0]


def step(value, n_expert):
    order = ring_order(n_expert // 2)
    follow = {at: order[(spot + 1) % len(order)] for spot, at in enumerate(order)}
    return lax.ppermute(value, "expert", [(2 * at + core, 2 * follow[at] + core) for at in order for core in range(2)])


def swap(value, n_expert):
    return lax.ppermute(value, "expert", [(at, at ^ 1) for at in range(n_expert)])


def flip(value, mask):
    return lax.ppermute(value, "dp", [(at, at ^ mask) for at in range(4)])


def add(*values):
    return sum(value.astype(F32) for value in values)


def slot_weights(expert_ids, gate_fixed, n_expert):
    gate_values = gate_fixed.astype(F32) / 65536.0
    experts = jnp.arange(n_expert, dtype=jnp.int32)[:, None, None]
    table = jnp.sum(jnp.where(expert_ids.T[None] == jnp.broadcast_to(experts, (n_expert, 1, 1)), gate_values.T[None], 0.0), axis=1)
    came = lax.all_to_all(table, "expert", split_axis=0, concat_axis=0, tiled=True)
    me = lax.axis_index("expert")
    order = ring_order(n_expert // 2)
    spot = sum(jnp.where(me // 2 == at, where, 0) for where, at in enumerate(order))
    rows = []
    for core in (0, 1):
        for slot in range(n_expert // 2):
            back = lax.rem(spot - slot + len(order), len(order))
            chip = sum(jnp.where(back == where, at, 0) for where, at in enumerate(order))
            rows.append(2 * chip + lax.rem(me + core, 2))
    source = jnp.stack(rows)
    return jnp.sum(jnp.where(source[:, None, None] == jnp.arange(n_expert)[None, :, None], came[None], 0.0), axis=1)


class Order:
    def __init__(self, start):
        self.last = start

    def point(self, *values):
        *values, self.last = lax.optimization_barrier((*values, self.last))
        return values

    def after(self, value):
        return lax.optimization_barrier((value, self.last))[0]


def dense_shards(tokens, cotangent, expert_ids, gate_fixed, w_gate, w_up, w_down):
    n_expert = lax.axis_size("expert")
    n, width = tokens.shape
    ff = w_gate.shape[2]
    half, cut = width // 2, width // 8

    def ring(value, name):
        with jax.named_scope(name):
            return step(order.after(value), n_expert)

    def twin(value, name):
        with jax.named_scope(name):
            return swap(order.after(value), n_expert)

    def flips(pair, masks, name):
        with jax.named_scope(name):
            return [flip(order.after(value), mask) for value, mask in zip(pair, masks)]

    def launch(name, kernel, outs, ins, scratch=(), smem=0):
        return call(name, kernel, outs, [*ins[:smem], order.after(ins[smem]), *ins[smem + 1 :]], scratch, smem)

    gate_w, up_w, down_w = w_gate[0].T, w_up[0].T, w_down[0]
    me = lax.axis_index("dp")
    offs = jnp.stack([((me ^ rel) * 2 + part) * (width // 8) for rel, part in PIECES]).astype(jnp.int32)

    def forward(slot, mine_a, mine_b, other_a, other_b):
        pair = 2 * n
        return launch(
            f"forward_{slot}",
            partial(forward_kernel, slot),
            [((pair, ff), BF16), ((pair, ff), F32), ((pair, ff), F32), ((n, width), BF16), ((n, width), BF16),
             ((pair, half), BF16), ((pair, half), BF16)],
            [offs, weights, mine_a, mine_b, other_a, other_b, gate_w, up_w, down_w],
            [((pair, width), BF16)],
            smem=1,
        )

    def row_grads(name, slots):
        return launch(
            name,
            partial(rows_kernel, slots),
            [((len(slots) * n, width), BF16)] * 2,
            [d_gate, d_up, gate_w, up_w],
        )

    def pick(value, which):
        return value[which * (n // 2) : (which + 1) * (n // 2)]

    def kept(mine, other, which=None):
        return add(mine, other) if which is None else add(pick(mine, which), pick(other, which))

    def split(name, value):
        return launch(name, split_kernel, [((value.shape[0], half), BF16)] * 2, [offs, value], smem=1)

    def grads(name, left, rights):
        return launch(name, grads_kernel, [((ff, half // 2), BF16)] * 2, [left, *rights], [((8 * n, half), BF16)])

    def cross(name, *pairs):
        count = len(pairs)
        *sums, near_a, near_b = launch(
            name,
            partial(cross_kernel, count),
            [((count, ff, cut), BF16)] * 2 + [((count, ff, cut), F32)] * 2,
            [value for came, own in pairs for value in (*came, *own)],
        )
        return sums, (near_a, near_b)

    def total(near, last, at):
        return jnp.concatenate([add(part[at], more[at]) for part, more in zip(near, last)], axis=1)

    def whole(part_a, part_b, mine, other):
        return jnp.concatenate(
            [add(part_a, kept(mine, other, 0)), add(part_b, kept(mine, other, 1))], axis=0
        ).astype(BF16)

    order = Order(jnp.zeros((8, 128), F32))
    a0, b0 = pick(tokens, 0), pick(tokens, 1)
    a1, b1 = ring(a0, "ta1"), ring(b0, "tb1")
    s0, k0 = split("split_cot", cotangent)
    s1 = ring(s0, "s1")
    ap0, bp0 = twin(a0, "ap0"), twin(b0, "bp0")
    weights = slot_weights(expert_ids, gate_fixed, n_expert)
    down_s, down_k = split("split_down", down_w)
    a1, s0, k0, weights, down_s, down_k = order.point(a1, s0, k0, weights, down_s, down_k)
    a2, ap1 = ring(a1, "ta2"), twin(a1, "ap1")
    (b1,) = order.point(b1)
    b2, bp1 = ring(b1, "tb2"), twin(b1, "bp1")
    (s1,) = order.point(s1)
    s2, sp0 = ring(s1, "s2"), twin(s0, "sp0")
    f0 = forward(0, a0, b0, ap0, bp0)
    a2, *f0 = order.point(a2, *f0)
    a3, ap2 = ring(a2, "ta3"), twin(a2, "ap2")
    (b2,) = order.point(b2)
    b3, bp2 = ring(b2, "tb3"), twin(b2, "bp2")
    f1 = forward(1, a1, b1, ap1, bp1)
    s2, *f1 = order.point(s2, *f1)
    s3, sp1 = ring(s2, "s3"), twin(s1, "sp1")
    o1 = twin(f1[4], "o1")
    (a3,) = order.point(a3)
    k1, ap3 = ring(k0, "k1"), twin(a3, "ap3")
    b3, o1 = order.point(b3, o1)
    bp3 = twin(b3, "bp3")
    m_a = ring(kept(f1[3], o1, 0).astype(BF16), "ma1")
    f2 = forward(2, a2, b2, ap2, bp2)
    s3, *f2 = order.point(s3, *f2)
    sp2, sp3, o2 = twin(s2, "sp2"), twin(s3, "sp3"), twin(f2[4], "o2")
    f3 = forward(3, a3, b3, ap3, bp3)
    k1, *f3 = order.point(k1, *f3)
    k2, kp0, kp1 = ring(k1, "k2"), twin(k0, "kp0"), twin(k1, "kp1")
    hids, facs_g, facs_u, outs_m = ([f[at] for f in (f0, f1, f2, f3)] for at in range(4))
    rows_s, rows_k = ([f[at] for f in (f0, f1, f2, f3)] for at in (5, 6))
    *sent, d_early = launch(
        "early",
        early_kernel,
        [((ff, half // 2), BF16)] * 2 + [((8 * n, ff), F32)],
        [weights, s0, s1, s2, s3, sp0, sp1, sp2, sp3, *hids, down_s],
        [((8 * n, half), BF16), ((8 * n, ff), BF16)],
    )
    m_a, o2, d_early, *sent = order.point(m_a, o2, d_early, *sent)
    down_came = flips(sent, (1, 2), "d1")
    m_a = ring(add(m_a, kept(outs_m[2], o2, 0)).astype(BF16), "ma2")
    o3 = twin(f3[4], "o3")
    (k2,) = order.point(k2)
    k3, kp2 = ring(k2, "k3"), twin(k2, "kp2")
    m_a, o3 = order.point(m_a, o3)
    m_a = ring(add(m_a, kept(outs_m[3], o3, 0)).astype(BF16), "ma3")
    (k3,) = order.point(k3)
    kp3 = twin(k3, "kp3")
    m_b = ring(kept(outs_m[1], o1, 1).astype(BF16), "mb1")
    d_gate, d_up, dy_k = launch(
        "late",
        late_kernel,
        [((8 * n, ff), BF16)] * 2 + [((8 * n, half), BF16)],
        [weights, k0, k1, k2, k3, kp0, kp1, kp2, kp3, *facs_g, *facs_u, d_early, down_k],
    )
    d_gate, d_up, dy_k, *down_came = order.point(d_gate, d_up, dy_k, *down_came)
    sent = grads("gate_s", d_gate, rows_s)
    d_up, m_a, *sent = order.point(d_up, m_a, *sent)
    gate_came = flips(sent, (1, 2), "g1")
    near_m, near_o = row_grads("rows_near", (1, 2))
    m_b, near_m, near_o, d_up = order.point(m_b, near_m, near_o, d_up)
    near_o = twin(near_o, "no")
    m_b = ring(add(m_b, kept(outs_m[2], o2, 1)).astype(BF16), "mb2")
    sent = grads("up_s", d_up, rows_s)
    d_gate, d_up, near_o, *sent = order.point(d_gate, d_up, near_o, *sent)
    up_came = flips(sent, (1, 2), "u1")
    g_a = ring(kept(near_m[:n], near_o[:n], 0).astype(BF16), "ga1")
    far_m, far_o = row_grads("rows_far", (3, 0))
    far_m, far_o, dy_k = order.point(far_m, far_o, dy_k)
    down_own = launch(
        "down_k", hidden_grads_kernel, [((ff, half // 2), BF16)] * 2, [dy_k, *hids], [((8 * n, ff), BF16)]
    )
    m_b, d_gate, *down_own = order.point(m_b, d_gate, *down_own)
    m_b = ring(add(m_b, kept(outs_m[3], o3, 1)).astype(BF16), "mb3")
    far_o, o0 = twin(far_o, "fo"), twin(f0[4], "o0")
    gate_own = grads("gate_k", d_gate, rows_k)
    g_a, d_up, *gate_own = order.point(g_a, d_up, *gate_own)
    g_a = ring(add(g_a, kept(near_m[n:], near_o[n:], 0)).astype(BF16), "ga2")
    g_b = ring(kept(near_m[:n], near_o[:n], 1).astype(BF16), "gb1")
    up_own = grads("up_k", d_up, rows_k)
    gate_came[0], gate_came[1], *up_own = order.point(*gate_came, *up_own)
    first_far, first_near = cross("first_cross", (down_came, down_own), (gate_came, gate_own))
    m_b, o0, *rest = order.point(m_b, o0, *first_far, *first_near)
    first_far, first_near = rest[:2], rest[2:]
    first_last = flips(first_far, (2, 1), "dg2")
    g_a, far_o = order.point(g_a, far_o)
    g_a = ring(add(g_a, kept(far_m[:n], far_o[:n], 0)).astype(BF16), "ga3")
    (g_b,) = order.point(g_b)
    g_b = ring(add(g_b, kept(near_m[n:], near_o[n:], 1)).astype(BF16), "gb2")
    mixed = whole(m_a, m_b, outs_m[0], o0)
    up_came = order.point(*up_came)
    up_far, up_near = cross("up_cross", (up_came, up_own))
    up_far = order.point(*up_far)
    up_last = flips(up_far, (2, 1), "u2")
    g_b, mixed = order.point(g_b, mixed)
    g_b = ring(add(g_b, kept(far_m[:n], far_o[:n], 1)).astype(BF16), "gb3")
    first_last = order.point(*first_last)
    grad_down, grad_gate = total(first_near, first_last, 0), total(first_near, first_last, 1)
    grad_up = total(up_near, up_last, 0)
    token_grad = whole(g_a, g_b, far_m[n:], far_o[n:])
    return (mixed, token_grad, grad_gate.T[None], grad_up.T[None], grad_down[None])


def shards(tokens, cotangent, expert_ids, gate_fixed, w_gate, w_up, w_down):
    n_expert = lax.axis_size("expert")
    rows, width = tokens.shape
    capacity = 4 * rows * expert_ids.shape[1] // (3 * n_expert)
    dense = capacity >= rows and n_expert == 8 and lax.axis_size("dp") == 4 and rows == 128 and width % 2048 == 0
    run = dense_shards if dense else slot_shards
    return run(tokens, cotangent, expert_ids, gate_fixed, w_gate, w_up, w_down)


def solution(mesh):
    in_specs = (
        P(("dp", "expert"), None),
        P(("dp", "expert"), None),
        P(("dp", "expert"), None),
        P(("dp", "expert"), None),
        P("expert", None, None),
        P("expert", None, None),
        P("expert", None, None),
    )
    out_specs = (
        P(("dp", "expert"), None),
        P(("dp", "expert"), None),
        P("expert", "dp", None),
        P("expert", "dp", None),
        P("expert", None, "dp"),
    )
    return jax.shard_map(shards, mesh=mesh, in_specs=in_specs, out_specs=out_specs, check_vma=False)
```

```python
from functools import partial

import jax
import jax.numpy as jnp
from jax import lax
from jax.experimental import pallas as pl
from jax.experimental.pallas import tpu as pltpu
from jax.sharding import PartitionSpec as P


def contract(left, right):
    return lax.dot_general(
        left, right, (((0,), (0,)), ((), ())), preferred_element_type=jnp.float32
    )


def trans_dot(left, right):
    return lax.dot_general(
        left, right, (((1,), (1,)), ((), ())), preferred_element_type=jnp.float32
    )


def forward_rows(gate_w, up_w, down_w, rows_in):
    gate_pre = jnp.dot(rows_in, gate_w, preferred_element_type=jnp.float32)
    up_pre = jnp.dot(rows_in, up_w, preferred_element_type=jnp.float32)
    hidden = (gate_pre * jax.nn.sigmoid(gate_pre) * up_pre).astype(jnp.bfloat16)
    expert_out = jnp.dot(hidden, down_w, preferred_element_type=jnp.float32).astype(jnp.bfloat16)
    return (expert_out, gate_pre, up_pre, hidden)


def backward_rows(gate_w, up_w, down_w, dy_rows, gate_pre, up_pre):
    sigma = jax.nn.sigmoid(gate_pre)
    activ = gate_pre * sigma
    d_hidden = trans_dot(dy_rows, down_w)
    d_gate = (d_hidden * up_pre * (sigma * (1.0 + gate_pre * (1.0 - sigma)))).astype(jnp.bfloat16)
    d_up = (d_hidden * activ).astype(jnp.bfloat16)
    d_rows = (trans_dot(d_gate, gate_w) + trans_dot(d_up, up_w)).astype(jnp.bfloat16)
    return (d_rows, d_gate, d_up)


def slot_shards(tokens, cotangent, expert_ids, gate_fixed, w_gate, w_up, w_down):
    n_expert = lax.axis_size("expert")
    tok_rows = tokens.shape[0]
    width = tokens.shape[1]
    top_k = expert_ids.shape[1]
    capacity = 4 * tok_rows * top_k // (3 * n_expert)
    slot_count = n_expert * capacity
    gate_w = w_gate[0]
    up_w = w_up[0]
    down_w = w_down[0]
    flat_ids = expert_ids.reshape(-1)
    onehot = (flat_ids[:, None] == jnp.arange(n_expert, dtype=jnp.int32)[None, :]).astype(jnp.int32)
    before = jnp.cumsum(onehot, axis=0) - onehot
    rank_in = jnp.sum(before * onehot, axis=1)
    counts = jnp.sum(onehot, axis=0)
    slot_of = flat_ids * capacity + rank_in
    owner = jnp.arange(flat_ids.shape[0], dtype=jnp.int32) // top_k
    slot_token = jnp.zeros((slot_count,), jnp.int32).at[slot_of].set(owner)
    gate_values = gate_fixed.reshape(-1).astype(jnp.float32) / 65536.0
    slot_gate = jnp.zeros((slot_count,), jnp.float32).at[slot_of].set(gate_values)
    outgoing = jnp.where(
        (slot_gate > 0.0)[:, None], tokens[slot_token], jnp.zeros((), tokens.dtype)
    )
    received, arrived = (
        lax.all_to_all(outgoing, "expert", split_axis=0, concat_axis=0, tiled=True),
        lax.all_to_all(counts, "expert", split_axis=0, concat_axis=0, tiled=True),
    )

    def run_rows(row_fn, inputs):
        return row_fn(*inputs)

    def fold_rows(left, right):
        return contract(left, right)

    expert_out, gate_pre, up_pre, hidden = run_rows(
        partial(forward_rows, gate_w, up_w, down_w), (received,)
    )
    returned = lax.all_to_all(expert_out, "expert", split_axis=0, concat_axis=0, tiled=True)
    mixed_rows = returned[slot_of].astype(jnp.float32).reshape(tok_rows, top_k, width)
    mixed = jnp.sum(mixed_rows * gate_values.reshape(tok_rows, top_k)[:, :, None], axis=1).astype(
        jnp.bfloat16
    )
    dy_out = (cotangent[slot_token].astype(jnp.float32) * slot_gate[:, None]).astype(jnp.bfloat16)
    dy_in = lax.all_to_all(dy_out, "expert", split_axis=0, concat_axis=0, tiled=True)
    d_rows, d_gate, d_up = run_rows(
        partial(backward_rows, gate_w, up_w, down_w), (dy_in, gate_pre, up_pre)
    )
    back_rows = lax.all_to_all(d_rows, "expert", split_axis=0, concat_axis=0, tiled=True)
    token_grad = jnp.sum(
        back_rows[slot_of].astype(jnp.float32).reshape(tok_rows, top_k, width), axis=1
    ).astype(jnp.bfloat16)
    grad_gate, grad_up, grad_down = (
        lax.psum_scatter(
            fold_rows(received, d_gate).astype(jnp.bfloat16), "dp", scatter_dimension=0, tiled=True
        ).astype(jnp.float32),
        lax.psum_scatter(
            fold_rows(received, d_up).astype(jnp.bfloat16), "dp", scatter_dimension=0, tiled=True
        ).astype(jnp.float32),
        lax.psum_scatter(
            fold_rows(hidden, dy_in).astype(jnp.bfloat16), "dp", scatter_dimension=1, tiled=True
        ).astype(jnp.float32),
    )
    return (mixed, token_grad, grad_gate[None], grad_up[None], grad_down[None])


BF16, F32 = jnp.bfloat16, jnp.float32
VMEM = pl.BlockSpec(memory_space=pltpu.VMEM)
SMEM = pl.BlockSpec(memory_space=pltpu.SMEM)
PIECES = ((1, 0), (3, 0), (2, 1), (3, 1), (0, 0), (2, 0), (0, 1), (1, 1))


def tie(*values):
    return lax.optimization_barrier(values)


def nt(left, right):
    return lax.dot_general(left, right, (((1,), (1,)), ((), ())), preferred_element_type=F32)


def nn(left, right):
    return lax.dot_general(left, right, (((1,), (0,)), ((), ())), preferred_element_type=F32)


def tn(left, right):
    return lax.dot_general(left, right, (((0,), (0,)), ((), ())), preferred_element_type=F32)


def call(name, kernel, outs, ins, scratch=(), smem=0, flops=1):
    return list(pl.pallas_call(
        kernel,
        name=name,
        out_shape=[jax.ShapeDtypeStruct(shape, dtype) for shape, dtype in outs],
        in_specs=[SMEM] * smem + [VMEM] * (len(ins) - smem),
        out_specs=[VMEM] * len(outs),
        scratch_shapes=[pltpu.VMEM(shape, dtype) for shape, dtype in scratch],
        compiler_params=pltpu.CompilerParams(vmem_limit_bytes=16 * 1024 * 1024),
        cost_estimate=pl.CostEstimate(flops=flops, bytes_accessed=1, transcendentals=0),
    )(*ins))


def per_row(weights, row, width):
    count = weights.shape[1]
    square = jnp.broadcast_to(weights[row : row + 1, :], (count, count)).T
    return jnp.concatenate([square] * (width // count), axis=1)


def forward_kernel(offs, *refs):
    parts, (gate, up, hid, fac_g, fac_u, rows_s, rows_k, rows) = refs[:-8], refs[-8:]
    size = rows.shape[1] // 8
    stack(parts, rows)
    gate_pre = nt(rows[...], gate[...])
    up_pre = nt(rows[...], up[...])
    sigma = jax.nn.sigmoid(gate_pre)
    activ = gate_pre * sigma
    hid[...] = (activ * up_pre).astype(BF16)
    fac_g[...] = up_pre * (sigma * (1.0 + gate_pre * (1.0 - sigma)))
    fac_u[...] = activ
    for at in range(8):
        here = pl.ds(pl.multiple_of(offs[at], size), size)
        (rows_s if at < 4 else rows_k)[:, pl.ds(at % 4 * size, size)] = rows[:, here]


def stack(parts, whole):
    at = 0
    for part in parts:
        whole[at : at + part.shape[0], :] = part[...]
        at += part.shape[0]


def backward_kernel(slot, offs, weights, hid, fac_g, fac_u, down, mine, *refs):
    others, (out_m, out_o, d_gate, d_up, dy_s, dy_k, dy) = refs[:-7], refs[-7:]
    n, width = mine.shape
    size = width // 8
    stack((mine, *others), dy)
    out = nn(hid[...], down[...])
    for at, (row, held) in enumerate(((slot, out_m), (slot + 4, out_o))):
        part = slice(at * n, (at + 1) * n)
        weight = per_row(weights[...], row, width)
        dy[part, :] = (dy[part, :].astype(F32) * weight).astype(BF16)
        held[...] = (out[part] * weight).astype(BF16)
    d_hid = nt(dy[...], down[...])
    d_gate[...] = (d_hid * fac_g[...]).astype(BF16)
    d_up[...] = (d_hid * fac_u[...]).astype(BF16)
    for at in range(8):
        here = pl.ds(pl.multiple_of(offs[at], size), size)
        (dy_s if at < 4 else dy_k)[:, pl.ds(at % 4 * size, size)] = dy[:, here]


def split_kernel(offs, whole, part_s, part_k):
    size = whole.shape[1] // 8
    for at in range(8):
        here = pl.ds(pl.multiple_of(offs[at], size), size)
        (part_s if at < 4 else part_k)[:, pl.ds(at % 4 * size, size)] = whole[:, here]


def weigh(slot, weights, parts, dy):
    stack(parts, dy)
    n = dy.shape[0] // 2
    for at, row in enumerate((slot, slot + 4)):
        part = slice(at * n, (at + 1) * n)
        dy[part, :] = (dy[part, :].astype(F32) * per_row(weights[...], row, dy.shape[1])).astype(BF16)


def early_kernel(weights, *refs):
    hids, dys, parts, (out_a, out_b, dy, left, right) = refs[:4], refs[4:7], refs[7:-5], refs[-5:]
    weigh(3, weights, parts, dy)
    stack(hids, left)
    stack((*dys, dy), right)
    half = right.shape[1] // 2
    out_a[0, :, :] = tn(left[...], right[:, :half]).astype(BF16)
    out_b[0, :, :] = tn(left[...], right[:, half:]).astype(BF16)


def out_kernel(slot, weights, hid, down, out_m, out_o):
    n, width = out_m.shape
    out = nn(hid[...], down[...])
    out_m[...] = (out[:n] * per_row(weights[...], slot, width)).astype(BF16)
    out_o[...] = (out[n:] * per_row(weights[...], slot + 4, width)).astype(BF16)


def sum_kernel(*refs):
    *parts, out = refs
    out[...] = sum(part[...].astype(F32) for part in parts).astype(BF16)


def last_kernel(offs, weights, fac_g, fac_u, down, dy_s, *refs):
    parts, (d_gate, d_up, dy_k, dy) = refs[:-4], refs[-4:]
    size = down.shape[1] // 8
    weigh(3, weights, parts, dy_k)
    for at in range(8):
        here = pl.ds(pl.multiple_of(offs[at], size), size)
        dy[:, here] = (dy_s if at < 4 else dy_k)[:, pl.ds(at % 4 * size, size)]
    d_hid = nt(dy[...], down[...])
    d_gate[...] = (d_hid * fac_g[...]).astype(BF16)
    d_up[...] = (d_hid * fac_u[...]).astype(BF16)


def grads_kernel(groups, *refs):
    ins, (out_a, out_b, left, right) = refs[:-4], refs[-4:]
    half = right.shape[1] // 2
    held = None
    for at, (first, second) in enumerate(groups):
        stack(ins[4 * first : 4 * first + 4], left)
        if second != held:
            stack(ins[4 * second : 4 * second + 4], right)
            held = second
        out_a[at, :, :] = tn(left[...], right[:, :half]).astype(BF16)
        out_b[at, :, :] = tn(left[...], right[:, half:]).astype(BF16)


def cross_kernel(came_a, came_b, down_a, down_b, own_a, own_b, far_a, far_b, near_a, near_b):
    cut = far_a.shape[2]
    for came, down, own, far, near in (
        (came_a, down_a, own_a, far_a, near_a),
        (came_b, down_b, own_b, far_b, near_b),
    ):
        for at in range(3):
            both = (down[0, :, :] if at == 2 else came[at, :, :]).astype(F32) + own[at, :, :].astype(F32)
            near[at, :, :] = both[:, :cut]
            far[at, :, :] = both[:, cut:].astype(BF16)


def finish_kernel(near_a, near_b, last_a, last_b, *outs):
    cut = near_a.shape[2]
    for at, out in enumerate(outs):
        out[:, :cut] = near_a[at, :, :] + last_a[at, :, :].astype(F32)
        out[:, cut:] = near_b[at, :, :] + last_b[at, :, :].astype(F32)


def rows_kernel(*refs):
    d_gate, d_up, gate, up, mine, *others = refs
    n = mine.shape[0]
    size = others[0].shape[0]
    both = nn(d_gate[...], gate[...]) + nn(d_up[...], up[...])
    mine[...] = both[:n].astype(BF16)
    for at, other in enumerate(others):
        other[...] = both[n + at * size : n + (at + 1) * size].astype(BF16)


def ring_order(count):
    return [0] + list(range(1, count, 2)) + [at for at in range(count - 1, 1, -1) if at % 2 == 0]


def step(value, n_expert):
    order = ring_order(n_expert // 2)
    follow = {at: order[(spot + 1) % len(order)] for spot, at in enumerate(order)}
    return lax.ppermute(value, "expert", [(2 * at + core, 2 * follow[at] + core) for at in order for core in range(2)])


def swap(value, n_expert):
    return lax.ppermute(value, "expert", [(at, at ^ 1) for at in range(n_expert)])


def flip(value, mask):
    return lax.ppermute(value, "dp", [(at, at ^ mask) for at in range(4)])


def add(*values):
    return sum(value.astype(F32) for value in values)


def slot_sources(n_expert):
    me = lax.axis_index("expert")
    order = ring_order(n_expert // 2)
    spot = sum(jnp.where(me // 2 == at, where, 0) for where, at in enumerate(order))
    rows = []
    for core in (0, 1):
        for slot in range(n_expert // 2):
            back = lax.rem(spot - slot + len(order), len(order))
            chip = sum(jnp.where(back == where, at, 0) for where, at in enumerate(order))
            rows.append(2 * chip + lax.rem(me + core, 2))
    return jnp.stack(rows).astype(jnp.int32)


def slot_weights(sources, expert_ids, gate_fixed, n_expert):
    gate_values = gate_fixed.astype(F32) / 65536.0
    experts = jnp.arange(n_expert, dtype=jnp.int32)[:, None, None]
    table = jnp.sum(jnp.where(expert_ids.T[None] == experts, gate_values.T[None], 0.0), axis=1)
    came = lax.all_to_all(table, "expert", split_axis=0, concat_axis=0, tiled=True)
    return jnp.sum(jnp.where(sources[:, None, None] == jnp.arange(n_expert)[None, :, None], came[None], 0.0), axis=1)


class Order:
    def __init__(self, start):
        self.last = start

    def point(self, *values):
        *values, self.last = lax.optimization_barrier((*values, self.last))
        return values

    def after(self, value):
        return lax.optimization_barrier((value, self.last))[0]


def dense_shards(tokens, cotangent, expert_ids, gate_fixed, w_gate, w_up, w_down):
    n_expert = lax.axis_size("expert")
    n, width = tokens.shape
    ff = w_gate.shape[2]
    half, cut = width // 2, width // 8

    def ring(value, name):
        with jax.named_scope(name):
            return step(order.after(value), n_expert)

    def twin(value, name):
        with jax.named_scope(name):
            return swap(order.after(value), n_expert)

    def flips(pair, masks, name):
        with jax.named_scope(name):
            return [flip(order.after(value), mask) for value, mask in zip(pair, masks)]

    def launch(name, kernel, outs, ins, scratch=(), smem=0, flops=1):
        return call(name, kernel, outs, [*ins[:smem], order.after(ins[smem]), *ins[smem + 1 :]], scratch, smem, flops)

    gate_w, up_w, down_w = w_gate[0].T, w_up[0].T, w_down[0]
    me = lax.axis_index("dp")
    offs = jnp.stack([((me ^ rel) * 2 + part) * (width // 8) for rel, part in PIECES]).astype(jnp.int32)

    def forward(slot, *parts):
        pair = 2 * n
        return launch(
            f"forward_{slot}",
            forward_kernel,
            [((pair, ff), BF16), ((pair, ff), F32), ((pair, ff), F32), ((pair, half), BF16), ((pair, half), BF16)],
            [offs, *parts, gate_w, up_w],
            [((pair, width), BF16)],
            smem=1,
        )

    def backward(slot, ahead, mine, *others):
        pair = 2 * n
        return launch(
            f"backward_{slot}",
            partial(backward_kernel, slot),
            [((n, width), BF16)] * 2 + [((pair, ff), BF16)] * 2 + [((pair, half), BF16)] * 2,
            [offs, weights, *ahead[:3], down_w, mine, *others],
            [((pair, width), BF16)],
            smem=1,
        )

    def grads(name, groups, *lists):
        return launch(
            name,
            partial(grads_kernel, groups),
            [((len(groups), ff, half // 2), BF16)] * 2,
            [part for parts in lists for part in parts],
            [((8 * n, ff), BF16), ((8 * n, half), BF16)],
        )

    def row_grads(name, slot, cuts=1):
        return launch(
            name,
            rows_kernel,
            [((n, width), BF16)] + [((n // cuts, width), BF16)] * cuts,
            [d_gates[slot], d_ups[slot], gate_w, up_w],
        )

    def pick(value, which):
        return value[which * (n // 2) : (which + 1) * (n // 2)]

    def kept(mine, other, which=None):
        return add(mine, other) if which is None else add(pick(mine, which), pick(other, which))

    def total(near, last, at):
        return jnp.concatenate([add(part[at], more[at]) for part, more in zip(near, last)], axis=1)

    def whole(part_a, part_b, mine, other):
        return jnp.concatenate(
            [add(part_a, kept(mine, other, 0)), add(part_b, kept(mine, other, 1))], axis=0
        ).astype(BF16)

    def twins(value, name):
        return [twin(pick(value, at), f"{name}_{at}") for at in range(2)]

    def early(*parts):
        return launch(
            "early",
            early_kernel,
            [((1, ff, half // 2), BF16)] * 2 + [((2 * n, half), BF16)],
            [weights, *hids, *dys_s, *parts],
            [((8 * n, ff), BF16), ((8 * n, half), BF16)],
        )

    def outputs(slot, hid):
        return launch(
            f"out_{slot}", partial(out_kernel, slot), [((n, width), BF16)] * 2, [weights, hid, down_w]
        )

    def backward_last(dy_s, *parts):
        return launch(
            "backward_3",
            last_kernel,
            [((2 * n, ff), BF16)] * 2 + [((2 * n, half), BF16)],
            [offs, weights, *f3[1:3], down_w, dy_s, *parts],
            [((2 * n, width), BF16)],
            smem=1,
        )

    def total_of(name, *parts):
        return launch(name, sum_kernel, [(parts[0].shape, BF16)], parts)[0]

    order = Order(jnp.zeros((8, 128), F32))
    sources = slot_sources(n_expert)
    t0, c0 = tokens, cotangent
    t1, c1 = ring(t0, "t1"), ring(c0, "c1")
    p0, q0 = twin(t0, "p0"), twin(c0, "q0")
    weights = slot_weights(sources, expert_ids, gate_fixed, n_expert)
    t1, weights = order.point(t1, weights)
    t2, p1 = ring(t1, "t2"), twin(t1, "p1")
    c1, p0 = order.point(c1, p0)
    c2, q1 = ring(c1, "c2"), twin(c1, "q1")
    f0 = forward(0, t0, p0)
    f1 = forward(1, t1, p1)
    t2, f0[0], f1[0] = order.point(t2, f0[0], f1[0])
    t3, p2 = ring(t2, "t3"), twin(t2, "p2")
    b0 = backward(0, f0, c0, q0)
    b1 = backward(1, f1, c1, q1)
    o1 = twin(b1[1], "o1")
    c2, b0[0], b1[0] = order.point(c2, b0[0], b1[0])
    c2s, c2k = launch("split", split_kernel, [((n, half), BF16)] * 2, [offs, c2], smem=1)
    c3s, c3k = ring(c2s, "c3s"), ring(c2k, "c3k")
    q2 = twins(c2, "q2")
    f2 = forward(2, t2, p2)
    b2 = backward(2, f2, c2, *q2)
    o2 = twin(b2[1], "o2")
    t3, o1, f2[0], b2[0] = order.point(t3, o1, f2[0], b2[0])
    p3 = twins(t3, "p3")
    c3s, o2 = order.point(c3s, o2)
    q3s = twins(c3s, "q3s")
    f3 = forward(3, t3, *p3)
    hids, facs_g, facs_u, rows_s, rows_k = ([f[at] for f in (f0, f1, f2, f3)] for at in range(5))
    dys_s = [b[4] for b in (b0, b1, b2)]
    *sent, dy3 = early(c3s, *q3s)
    dy3, *sent = order.point(dy3, *sent)
    down_came = flips(sent, (1, 2), "d1")
    m = ring(total_of("add_m1", b1[0], o1), "m1")
    out3 = outputs(3, f3[0])
    (c3k,) = order.point(c3k)
    q3k = twin(c3k, "q3k")
    b3 = backward_last(dy3, c3k, q3k)
    b3 = [*out3, *b3[:2], dy3, b3[2]]
    outs_m, outs_o, d_gates, d_ups, dys_s, dys_k = ([b[at] for b in (b0, b1, b2, b3)] for at in range(6))
    sent = grads("both_s", ((0, 2), (1, 2)), d_gates, d_ups, rows_s)
    d_gates[1], *sent = order.point(d_gates[1], *sent)
    m1, r1 = row_grads("rows_1", 1)
    m, d_gates[2], r1 = order.point(m, d_gates[2], r1)
    m = ring(total_of("add_m2", m, outs_m[2], o2), "m2")
    r1, o3 = twin(r1, "r1"), twin(outs_o[3], "o3")
    m2, r2 = row_grads("rows_2", 2)
    m3, r3 = row_grads("rows_3", 3)
    m0, r0 = row_grads("rows_0", 0)
    r1, o3, r2, r3, r0, d_gates[0], *down_came = order.point(r1, o3, r2, r3, r0, d_gates[0], *down_came)
    both_came = flips(sent, (1, 2), "gu1")
    g = ring(total_of("add_g1", m1, r1), "ga1")
    own = grads("kept_k", ((0, 2), (1, 2), (3, 4)), d_gates, d_ups, rows_k, hids, dys_k)
    o0 = twin(outs_o[0], "o0")
    m, o0, *own = order.point(m, o0, *own)
    m = ring(total_of("add_m3", m, outs_m[3], o3), "m3")
    r2 = twin(r2, "r2")
    g, r2 = order.point(g, r2)
    g = ring(total_of("add_g2", g, m2, r2), "ga2")
    r3 = twin(r3, "r3")
    both_came = order.point(*both_came)
    *far, near_a, near_b = launch(
        "cross",
        cross_kernel,
        [((3, ff, cut), BF16)] * 2 + [((3, ff, cut), F32)] * 2,
        [*both_came, *down_came, *own],
    )
    far = order.point(*far)
    last = flips(far, (2, 1), "last")
    g, r3, m = order.point(g, r3, m)
    g = ring(add(g, kept(m3, r3)).astype(BF16), "ga3")
    r0 = twin(r0, "r0")
    mixed = total_of("add_m0", m, outs_m[0], o0)
    mixed, r0, g = order.point(mixed, r0, g)
    token_grad = add(g, kept(m0, r0)).astype(BF16)
    token_grad, *last = order.point(token_grad, *last)
    grad_gate, grad_up, grad_down = launch(
        "finish", finish_kernel, [((ff, 2 * cut), F32)] * 3, [near_a, near_b, *last]
    )
    return (mixed, token_grad, grad_gate.T[None], grad_up.T[None], grad_down[None])


def shards(tokens, cotangent, expert_ids, gate_fixed, w_gate, w_up, w_down):
    n_expert = lax.axis_size("expert")
    rows, width = tokens.shape
    capacity = 4 * rows * expert_ids.shape[1] // (3 * n_expert)
    dense = capacity >= rows and n_expert == 8 and lax.axis_size("dp") == 4 and rows == 128 and width % 2048 == 0
    run = dense_shards if dense else slot_shards
    return run(tokens, cotangent, expert_ids, gate_fixed, w_gate, w_up, w_down)


def solution(mesh):
    in_specs = (
        P(("dp", "expert"), None),
        P(("dp", "expert"), None),
        P(("dp", "expert"), None),
        P(("dp", "expert"), None),
        P("expert", None, None),
        P("expert", None, None),
        P("expert", None, None),
    )
    out_specs = (
        P(("dp", "expert"), None),
        P(("dp", "expert"), None),
        P("expert", "dp", None),
        P("expert", "dp", None),
        P("expert", None, "dp"),
    )
    return jax.shard_map(shards, mesh=mesh, in_specs=in_specs, out_specs=out_specs, check_vma=False)
```

```python
from functools import partial

import jax
import jax.numpy as jnp
from jax import lax
from jax.experimental import pallas as pl
from jax.experimental.pallas import tpu as pltpu
from jax.sharding import PartitionSpec as P


def contract(left, right):
    return lax.dot_general(
        left, right, (((0,), (0,)), ((), ())), preferred_element_type=jnp.float32
    )


def trans_dot(left, right):
    return lax.dot_general(
        left, right, (((1,), (1,)), ((), ())), preferred_element_type=jnp.float32
    )


def forward_rows(gate_w, up_w, down_w, rows_in):
    gate_pre = jnp.dot(rows_in, gate_w, preferred_element_type=jnp.float32)
    up_pre = jnp.dot(rows_in, up_w, preferred_element_type=jnp.float32)
    hidden = (gate_pre * jax.nn.sigmoid(gate_pre) * up_pre).astype(jnp.bfloat16)
    expert_out = jnp.dot(hidden, down_w, preferred_element_type=jnp.float32).astype(jnp.bfloat16)
    return (expert_out, gate_pre, up_pre, hidden)


def backward_rows(gate_w, up_w, down_w, dy_rows, gate_pre, up_pre):
    sigma = jax.nn.sigmoid(gate_pre)
    activ = gate_pre * sigma
    d_hidden = trans_dot(dy_rows, down_w)
    d_gate = (d_hidden * up_pre * (sigma * (1.0 + gate_pre * (1.0 - sigma)))).astype(jnp.bfloat16)
    d_up = (d_hidden * activ).astype(jnp.bfloat16)
    d_rows = (trans_dot(d_gate, gate_w) + trans_dot(d_up, up_w)).astype(jnp.bfloat16)
    return (d_rows, d_gate, d_up)


def slot_shards(tokens, cotangent, expert_ids, gate_fixed, w_gate, w_up, w_down):
    n_expert = lax.axis_size("expert")
    tok_rows = tokens.shape[0]
    width = tokens.shape[1]
    top_k = expert_ids.shape[1]
    capacity = 4 * tok_rows * top_k // (3 * n_expert)
    slot_count = n_expert * capacity
    gate_w = w_gate[0]
    up_w = w_up[0]
    down_w = w_down[0]
    flat_ids = expert_ids.reshape(-1)
    onehot = (flat_ids[:, None] == jnp.arange(n_expert, dtype=jnp.int32)[None, :]).astype(jnp.int32)
    before = jnp.cumsum(onehot, axis=0) - onehot
    rank_in = jnp.sum(before * onehot, axis=1)
    counts = jnp.sum(onehot, axis=0)
    slot_of = flat_ids * capacity + rank_in
    owner = jnp.arange(flat_ids.shape[0], dtype=jnp.int32) // top_k
    slot_token = jnp.zeros((slot_count,), jnp.int32).at[slot_of].set(owner)
    gate_values = gate_fixed.reshape(-1).astype(jnp.float32) / 65536.0
    slot_gate = jnp.zeros((slot_count,), jnp.float32).at[slot_of].set(gate_values)
    outgoing = jnp.where(
        (slot_gate > 0.0)[:, None], tokens[slot_token], jnp.zeros((), tokens.dtype)
    )
    received, arrived = (
        lax.all_to_all(outgoing, "expert", split_axis=0, concat_axis=0, tiled=True),
        lax.all_to_all(counts, "expert", split_axis=0, concat_axis=0, tiled=True),
    )

    def run_rows(row_fn, inputs):
        return row_fn(*inputs)

    def fold_rows(left, right):
        return contract(left, right)

    expert_out, gate_pre, up_pre, hidden = run_rows(
        partial(forward_rows, gate_w, up_w, down_w), (received,)
    )
    returned = lax.all_to_all(expert_out, "expert", split_axis=0, concat_axis=0, tiled=True)
    mixed_rows = returned[slot_of].astype(jnp.float32).reshape(tok_rows, top_k, width)
    mixed = jnp.sum(mixed_rows * gate_values.reshape(tok_rows, top_k)[:, :, None], axis=1).astype(
        jnp.bfloat16
    )
    dy_out = (cotangent[slot_token].astype(jnp.float32) * slot_gate[:, None]).astype(jnp.bfloat16)
    dy_in = lax.all_to_all(dy_out, "expert", split_axis=0, concat_axis=0, tiled=True)
    d_rows, d_gate, d_up = run_rows(
        partial(backward_rows, gate_w, up_w, down_w), (dy_in, gate_pre, up_pre)
    )
    back_rows = lax.all_to_all(d_rows, "expert", split_axis=0, concat_axis=0, tiled=True)
    token_grad = jnp.sum(
        back_rows[slot_of].astype(jnp.float32).reshape(tok_rows, top_k, width), axis=1
    ).astype(jnp.bfloat16)
    grad_gate, grad_up, grad_down = (
        lax.psum_scatter(
            fold_rows(received, d_gate).astype(jnp.bfloat16), "dp", scatter_dimension=0, tiled=True
        ).astype(jnp.float32),
        lax.psum_scatter(
            fold_rows(received, d_up).astype(jnp.bfloat16), "dp", scatter_dimension=0, tiled=True
        ).astype(jnp.float32),
        lax.psum_scatter(
            fold_rows(hidden, dy_in).astype(jnp.bfloat16), "dp", scatter_dimension=1, tiled=True
        ).astype(jnp.float32),
    )
    return (mixed, token_grad, grad_gate[None], grad_up[None], grad_down[None])


BF16, F32 = jnp.bfloat16, jnp.float32
VMEM = pl.BlockSpec(memory_space=pltpu.VMEM)
SMEM = pl.BlockSpec(memory_space=pltpu.SMEM)
PIECES = ((1, 0), (3, 0), (2, 1), (3, 1), (0, 0), (2, 0), (0, 1), (1, 1))


def tie(*values):
    return lax.optimization_barrier(values)


def nt(left, right):
    return lax.dot_general(left, right, (((1,), (1,)), ((), ())), preferred_element_type=F32)


def nn(left, right):
    return lax.dot_general(left, right, (((1,), (0,)), ((), ())), preferred_element_type=F32)


def tn(left, right):
    return lax.dot_general(left, right, (((0,), (0,)), ((), ())), preferred_element_type=F32)


def call(name, kernel, outs, ins, scratch=(), smem=0, flops=1):
    return list(pl.pallas_call(
        kernel,
        name=name,
        out_shape=[jax.ShapeDtypeStruct(shape, dtype) for shape, dtype in outs],
        in_specs=[SMEM] * smem + [VMEM] * (len(ins) - smem),
        out_specs=[VMEM] * len(outs),
        scratch_shapes=[pltpu.VMEM(shape, dtype) for shape, dtype in scratch],
        compiler_params=pltpu.CompilerParams(vmem_limit_bytes=16 * 1024 * 1024),
        cost_estimate=pl.CostEstimate(flops=flops, bytes_accessed=1, transcendentals=0),
    )(*ins))


def pack_kernel(ids, gates, cot, out):
    n, width = cot.shape
    column = lax.broadcasted_iota(jnp.int32, (n, 128), 1)
    extra = jnp.zeros((n, 128), jnp.int32)
    for at in range(ids.shape[1]):
        expert, gate = ids[:, at : at + 1], gates[:, at : at + 1]
        extra += jnp.where(column == expert, gate >> 8, 0)
        extra += jnp.where(column == expert + 8, gate & 255, 0)
    out[:, :width] = cot[...]
    out[:, width:] = extra.astype(F32).astype(BF16)


def gate_column(expert, extra):
    column = lax.broadcasted_iota(jnp.int32, extra.shape, 1)
    scale = jnp.where(column == expert, 256.0, jnp.where(column == expert + 8, 1.0, 0.0))
    return jnp.sum(extra.astype(F32) * scale, axis=1, keepdims=True) / 65536.0


def forward_kernel(offs, *refs):
    parts, (gate, up, hid, fac_g, fac_u, rows_s, rows_k, rows) = refs[:-8], refs[-8:]
    size = rows.shape[1] // 8
    stack(parts, rows)
    gate_pre = nt(rows[...], gate[...])
    up_pre = nt(rows[...], up[...])
    sigma = jax.nn.sigmoid(gate_pre)
    activ = gate_pre * sigma
    hid[...] = (activ * up_pre).astype(BF16)
    fac_g[...] = up_pre * (sigma * (1.0 + gate_pre * (1.0 - sigma)))
    fac_u[...] = activ
    for at in range(8):
        here = pl.ds(pl.multiple_of(offs[at], size), size)
        (rows_s if at < 4 else rows_k)[:, pl.ds(at % 4 * size, size)] = rows[:, here]


def stack(parts, whole):
    at = 0
    for part in parts:
        whole[at : at + part.shape[0], :] = part[...]
        at += part.shape[0]


def backward_kernel(offs, hid, fac_g, fac_u, down, *refs):
    parts, (out_m, out_o, d_gate, d_up, dy_s, dy_k, held, dy) = refs[:-8], refs[-8:]
    n, width = out_m.shape
    size = width // 8
    stack(parts, held)
    out = nn(hid[...], down[...])
    for at, result in enumerate((out_m, out_o)):
        part = slice(at * n, (at + 1) * n)
        gate = gate_column(offs[8], held[part, width:])
        dy[part, :] = (held[part, :width].astype(F32) * gate).astype(BF16)
        result[...] = (out[part] * gate).astype(BF16)
    d_hid = nt(dy[...], down[...])
    d_gate[...] = (d_hid * fac_g[...]).astype(BF16)
    d_up[...] = (d_hid * fac_u[...]).astype(BF16)
    for at in range(8):
        here = pl.ds(pl.multiple_of(offs[at], size), size)
        (dy_s if at < 4 else dy_k)[:, pl.ds(at % 4 * size, size)] = dy[:, here]


def split_kernel(offs, whole, part_s, part_k):
    width = 2 * part_k.shape[1]
    size = width // 8
    for at in range(8):
        here = pl.ds(pl.multiple_of(offs[at], size), size)
        (part_s if at < 4 else part_k)[:, pl.ds(at % 4 * size, size)] = whole[:, here]
    part_s[:, width // 2 :] = whole[:, width:]


def early_kernel(offs, *refs):
    hids, dys, parts, (out_a, out_b, dy, gates, held, left, right) = refs[:4], refs[4:7], refs[7:-7], refs[-7:]
    stack(parts, held)
    half = dy.shape[1]
    gate = gate_column(offs[8], held[:, half:])
    gates[...] = jnp.broadcast_to(gate, gates.shape)
    dy[...] = (held[:, :half].astype(F32) * gate).astype(BF16)
    stack(hids, left)
    stack((*dys, dy), right)
    out_a[0, :, :] = tn(left[...], right[:, : half // 2]).astype(BF16)
    out_b[0, :, :] = tn(left[...], right[:, half // 2 :]).astype(BF16)


def out_kernel(hid, down, gates, out_m, out_o):
    n = out_m.shape[0]
    out = nn(hid[...], down[...]) * gates[:, :1]
    out_m[...] = out[:n].astype(BF16)
    out_o[...] = out[n:].astype(BF16)


def sum_kernel(spec, *refs):
    *parts, out = refs
    total, at = 0.0, 0
    for count, low in spec:
        if count == 1:
            term = parts[at][low : low + out.shape[0], :]
        else:
            term = jnp.concatenate([part[...] for part in parts[at : at + count]], axis=0)
        total = total + term.astype(F32)
        at += count
    out[...] = total.astype(BF16)


def last_kernel(offs, gates, fac_g, fac_u, down, dy_s, *refs):
    parts, (d_gate, d_up, dy_k, dy) = refs[:-4], refs[-4:]
    size = down.shape[1] // 8
    stack(parts, dy_k)
    dy_k[...] = (dy_k[...].astype(F32) * gates[:, :1]).astype(BF16)
    for at in range(8):
        here = pl.ds(pl.multiple_of(offs[at], size), size)
        dy[:, here] = (dy_s if at < 4 else dy_k)[:, pl.ds(at % 4 * size, size)]
    d_hid = nt(dy[...], down[...])
    d_gate[...] = (d_hid * fac_g[...]).astype(BF16)
    d_up[...] = (d_hid * fac_u[...]).astype(BF16)


def grads_kernel(groups, *refs):
    ins, (out_a, out_b, left, right) = refs[:-4], refs[-4:]
    half = right.shape[1] // 2
    held = None
    for at, (first, second) in enumerate(groups):
        stack(ins[4 * first : 4 * first + 4], left)
        if second != held:
            stack(ins[4 * second : 4 * second + 4], right)
            held = second
        out_a[at, :, :] = tn(left[...], right[:, :half]).astype(BF16)
        out_b[at, :, :] = tn(left[...], right[:, half:]).astype(BF16)


def cross_kernel(came_a, came_b, down_a, down_b, own_a, own_b, far_a, far_b, near_a, near_b):
    cut = far_a.shape[2]
    for came, down, own, far, near in (
        (came_a, down_a, own_a, far_a, near_a),
        (came_b, down_b, own_b, far_b, near_b),
    ):
        for at in range(3):
            both = (down[0, :, :] if at == 2 else came[at, :, :]).astype(F32) + own[at, :, :].astype(F32)
            near[at, :, :] = both[:, :cut]
            far[at, :, :] = both[:, cut:].astype(BF16)


def finish_kernel(near_a, near_b, last_a, last_b, *outs):
    cut = near_a.shape[2]
    for at, out in enumerate(outs):
        out[:, :cut] = near_a[at, :, :] + last_a[at, :, :].astype(F32)
        out[:, cut:] = near_b[at, :, :] + last_b[at, :, :].astype(F32)


def rows_kernel(*refs):
    d_gate, d_up, gate, up, mine, *others = refs
    n = mine.shape[0]
    size = others[0].shape[0]
    both = nn(d_gate[...], gate[...]) + nn(d_up[...], up[...])
    mine[...] = both[:n].astype(BF16)
    for at, other in enumerate(others):
        other[...] = both[n + at * size : n + (at + 1) * size].astype(BF16)


def ring_order(count):
    return [0] + list(range(1, count, 2)) + [at for at in range(count - 1, 1, -1) if at % 2 == 0]


def step(value, n_expert):
    order = ring_order(n_expert // 2)
    follow = {at: order[(spot + 1) % len(order)] for spot, at in enumerate(order)}
    return lax.ppermute(value, "expert", [(2 * at + core, 2 * follow[at] + core) for at in order for core in range(2)])


def swap(value, n_expert):
    return lax.ppermute(value, "expert", [(at, at ^ 1) for at in range(n_expert)])


def flip(value, mask):
    return lax.ppermute(value, "dp", [(at, at ^ mask) for at in range(4)])


def add(*values):
    return sum(value.astype(F32) for value in values)


class Order:
    def __init__(self, start):
        self.last = start

    def point(self, *values):
        *values, self.last = lax.optimization_barrier((*values, self.last))
        return values

    def after(self, value):
        return lax.optimization_barrier((value, self.last))[0]


def dense_shards(tokens, cotangent, expert_ids, gate_fixed, w_gate, w_up, w_down):
    n_expert = lax.axis_size("expert")
    n, width = tokens.shape
    ff = w_gate.shape[2]
    half, cut = width // 2, width // 8

    def ring(value, name):
        with jax.named_scope(name):
            return step(order.after(value), n_expert)

    def twin(value, name):
        with jax.named_scope(name):
            return swap(order.after(value), n_expert)

    def flips(pair, masks, name):
        with jax.named_scope(name):
            return [flip(order.after(value), mask) for value, mask in zip(pair, masks)]

    def launch(name, kernel, outs, ins, scratch=(), smem=0, flops=1):
        return call(name, kernel, outs, [*ins[:smem], order.after(ins[smem]), *ins[smem + 1 :]], scratch, smem, flops)

    gate_w, up_w, down_w = w_gate[0].T, w_up[0].T, w_down[0]
    me = lax.axis_index("dp")
    offs = [((me ^ rel) * 2 + part) * (width // 8) for rel, part in PIECES]
    offs = jnp.stack([*offs, lax.axis_index("expert")]).astype(jnp.int32)

    def forward(slot, *parts):
        pair = 2 * n
        return launch(
            f"forward_{slot}",
            forward_kernel,
            [((pair, ff), BF16), ((pair, ff), F32), ((pair, ff), F32), ((pair, half), BF16), ((pair, half), BF16)],
            [offs, *parts, gate_w, up_w],
            [((pair, width), BF16)],
            smem=1,
        )

    def backward(slot, ahead, *parts):
        pair = 2 * n
        return launch(
            f"backward_{slot}",
            backward_kernel,
            [((n, width), BF16)] * 2 + [((pair, ff), BF16)] * 2 + [((pair, half), BF16)] * 2,
            [offs, *ahead[:3], down_w, *parts],
            [((pair, width + 128), BF16), ((pair, width), BF16)],
            smem=1,
        )

    def grads(name, groups, *lists):
        return launch(
            name,
            partial(grads_kernel, groups),
            [((len(groups), ff, half // 2), BF16)] * 2,
            [part for parts in lists for part in parts],
            [((8 * n, ff), BF16), ((8 * n, half), BF16)],
        )

    def row_grads(name, slot, cuts=1):
        return launch(
            name,
            rows_kernel,
            [((n, width), BF16)] + [((n // cuts, width), BF16)] * cuts,
            [d_gates[slot], d_ups[slot], gate_w, up_w],
        )

    def pick(value, which):
        return value[which * (n // 2) : (which + 1) * (n // 2)]

    def kept(mine, other, which=None):
        return add(mine, other) if which is None else add(pick(mine, which), pick(other, which))

    def total(near, last, at):
        return jnp.concatenate([add(part[at], more[at]) for part, more in zip(near, last)], axis=1)

    def whole(part_a, part_b, mine, other):
        return jnp.concatenate(
            [add(part_a, kept(mine, other, 0)), add(part_b, kept(mine, other, 1))], axis=0
        ).astype(BF16)

    def twins(value, name):
        return [twin(pick(value, at), f"{name}_{at}") for at in range(2)]

    def early(*parts):
        return launch(
            "early",
            early_kernel,
            [((1, ff, half // 2), BF16)] * 2 + [((2 * n, half), BF16), ((2 * n, 128), F32)],
            [offs, *hids, *dys_s, *parts],
            [((2 * n, half + 128), BF16), ((8 * n, ff), BF16), ((8 * n, half), BF16)],
            smem=1,
        )

    def outputs(name, hid, gates):
        return launch(name, out_kernel, [((n, width), BF16)] * 2, [hid, down_w, gates])

    def backward_last(gates, dy_s, *parts):
        return launch(
            "backward_3",
            last_kernel,
            [((2 * n, ff), BF16)] * 2 + [((2 * n, half), BF16)],
            [offs, gates, *f3[1:3], down_w, dy_s, *parts],
            [((2 * n, width), BF16)],
            smem=1,
        )

    def sums(name, *terms, rows=n, low=0):
        terms = [term if isinstance(term, list) else [term] for term in terms]
        spec = tuple((len(term), low if term[0].shape[0] > rows else 0) for term in terms)
        ins = [part for term in terms for part in term]
        return launch(name, partial(sum_kernel, spec), [((rows, width), BF16)], ins)[0]

    order = Order(jnp.zeros((8, 128), F32))
    t0 = tokens
    t1, p0 = ring(t0, "t1"), twin(t0, "p0")
    c0 = launch("pack", pack_kernel, [((n, width + 128), BF16)], [expert_ids, gate_fixed, cotangent])[0]
    c1, q0 = ring(c0, "c1"), twin(c0, "q0")
    (t1,) = order.point(t1)
    t2, p1 = ring(t1, "t2"), twin(t1, "p1")
    c1, p0, p1 = order.point(c1, p0, p1)
    c2, q1 = ring(c1, "c2"), twin(c1, "q1")
    f0 = forward(0, t0, p0)
    f1 = forward(1, t1, p1)
    t2, f0[0], f1[0] = order.point(t2, f0[0], f1[0])
    t3, p2 = ring(t2, "t3"), twin(t2, "p2")
    b0 = backward(0, f0, c0, q0)
    b1 = backward(1, f1, c1, q1)
    o1 = twin(b1[1], "o1")
    c2, p2, b0[0], b1[0] = order.point(c2, p2, b0[0], b1[0])
    c2s, c2k = launch("split", split_kernel, [((n, half + 128), BF16), ((n, half), BF16)], [offs, c2], smem=1)
    c3s = ring(c2s, "c3s")
    q2 = twins(c2, "q2")
    f2 = forward(2, t2, p2)
    b2 = backward(2, f2, c2, *q2)
    o2 = twin(b2[1], "o2")
    t3, o1, f2[0], b2[0] = order.point(t3, o1, f2[0], b2[0])
    c3k = ring(c2k, "c3k")
    p3 = twins(t3, "p3")
    m = ring(sums("add_m1", b1[0], o1), "m1")
    c3s, o2 = order.point(c3s, o2)
    q3s = twins(c3s, "q3s")
    f3 = forward(3, t3, *p3)
    hids, facs_g, facs_u, rows_s, rows_k = ([f[at] for f in (f0, f1, f2, f3)] for at in range(5))
    dys_s = [b[4] for b in (b0, b1, b2)]
    *sent, dy3, gates3 = early(c3s, *q3s)
    dy3, *sent = order.point(dy3, *sent)
    down_came = flips(sent, (1, 2), "d1")
    out3 = outputs("out_3", f3[0], gates3)
    (c3k,) = order.point(c3k)
    q3k = twins(c3k, "q3k")
    b3 = backward_last(gates3, dy3, c3k, *q3k)
    b3 = [*out3, *b3[:2], dy3, b3[2]]
    outs_m, outs_o, d_gates, d_ups, dys_s, dys_k = ([b[at] for b in (b0, b1, b2, b3)] for at in range(6))
    sent = grads("both_s", ((0, 2), (1, 2)), d_gates, d_ups, rows_s)
    d_gates[1], *sent = order.point(d_gates[1], *sent)
    m1, r1 = row_grads("rows_1", 1)
    m, d_gates[2], r1 = order.point(m, d_gates[2], r1)
    m = ring(sums("add_m2", m, outs_m[2], o2), "m2")
    r1, o3 = twin(r1, "r1"), twin(outs_o[3], "o3")
    r1, o3, d_gates[0], *down_came = order.point(r1, o3, d_gates[0], *down_came)
    both_came = flips(sent, (1, 2), "gu1")
    g = ring(sums("add_g1", m1, r1), "ga1")
    o0 = twin(outs_o[0], "o0")
    m2, r2 = row_grads("rows_2", 2)
    m3, r3 = row_grads("rows_3", 3)
    m0, r0 = row_grads("rows_0", 0)
    own = grads("kept_k", ((0, 2), (1, 2), (3, 4)), d_gates, d_ups, rows_k, hids, dys_k)
    m, o0, m2, r2, m3, r3, m0, r0, *own = order.point(m, o0, m2, r2, m3, r3, m0, r0, *own)
    m = ring(sums("add_m3", m, outs_m[3], o3), "m3")
    r2 = twin(r2, "r2")
    g, r2 = order.point(g, r2)
    g = ring(sums("add_g2", g, m2, r2), "ga2")
    r3 = twin(r3, "r3")
    both_came[0], both_came[1], m = order.point(*both_came, m)
    *far, near_a, near_b = launch(
        "cross",
        cross_kernel,
        [((3, ff, cut), BF16)] * 2 + [((3, ff, cut), F32)] * 2,
        [*both_came, *down_came, *own],
    )
    far = order.point(*far)
    last = flips(far, (2, 1), "last")
    g, r3 = order.point(g, r3)
    g = ring(add(g, kept(m3, r3)).astype(BF16), "ga3")
    r0 = twin(r0, "r0")
    mixed = sums("add_m0", m, outs_m[0], o0)
    g, r0, mixed = order.point(g, r0, mixed)
    token_grad = add(g, kept(m0, r0)).astype(BF16)
    token_grad, *last = order.point(token_grad, *last)
    grad_gate, grad_up, grad_down = launch(
        "finish", finish_kernel, [((ff, 2 * cut), F32)] * 3, [near_a, near_b, *last]
    )
    return (mixed, token_grad, grad_gate.T[None], grad_up.T[None], grad_down[None])


def shards(tokens, cotangent, expert_ids, gate_fixed, w_gate, w_up, w_down):
    n_expert = lax.axis_size("expert")
    rows, width = tokens.shape
    capacity = 4 * rows * expert_ids.shape[1] // (3 * n_expert)
    dense = capacity >= rows and n_expert == 8 and lax.axis_size("dp") == 4 and rows == 128 and width % 2048 == 0
    run = dense_shards if dense else slot_shards
    return run(tokens, cotangent, expert_ids, gate_fixed, w_gate, w_up, w_down)


def solution(mesh):
    in_specs = (
        P(("dp", "expert"), None),
        P(("dp", "expert"), None),
        P(("dp", "expert"), None),
        P(("dp", "expert"), None),
        P("expert", None, None),
        P("expert", None, None),
        P("expert", None, None),
    )
    out_specs = (
        P(("dp", "expert"), None),
        P(("dp", "expert"), None),
        P("expert", "dp", None),
        P("expert", "dp", None),
        P("expert", None, "dp"),
    )
    return jax.shard_map(shards, mesh=mesh, in_specs=in_specs, out_specs=out_specs, check_vma=False)
```

```python
from functools import partial

import jax
import jax.numpy as jnp
from jax import lax
from jax.experimental import pallas as pl
from jax.experimental.pallas import tpu as pltpu
from jax.sharding import PartitionSpec as P


def contract(left, right):
    return lax.dot_general(
        left, right, (((0,), (0,)), ((), ())), preferred_element_type=jnp.float32
    )


def trans_dot(left, right):
    return lax.dot_general(
        left, right, (((1,), (1,)), ((), ())), preferred_element_type=jnp.float32
    )


def forward_rows(gate_w, up_w, down_w, rows_in):
    gate_pre = jnp.dot(rows_in, gate_w, preferred_element_type=jnp.float32)
    up_pre = jnp.dot(rows_in, up_w, preferred_element_type=jnp.float32)
    hidden = (gate_pre * jax.nn.sigmoid(gate_pre) * up_pre).astype(jnp.bfloat16)
    expert_out = jnp.dot(hidden, down_w, preferred_element_type=jnp.float32).astype(jnp.bfloat16)
    return (expert_out, gate_pre, up_pre, hidden)


def backward_rows(gate_w, up_w, down_w, dy_rows, gate_pre, up_pre):
    sigma = jax.nn.sigmoid(gate_pre)
    activ = gate_pre * sigma
    d_hidden = trans_dot(dy_rows, down_w)
    d_gate = (d_hidden * up_pre * (sigma * (1.0 + gate_pre * (1.0 - sigma)))).astype(jnp.bfloat16)
    d_up = (d_hidden * activ).astype(jnp.bfloat16)
    d_rows = (trans_dot(d_gate, gate_w) + trans_dot(d_up, up_w)).astype(jnp.bfloat16)
    return (d_rows, d_gate, d_up)


def slot_shards(tokens, cotangent, expert_ids, gate_fixed, w_gate, w_up, w_down):
    n_expert = lax.axis_size("expert")
    tok_rows = tokens.shape[0]
    width = tokens.shape[1]
    top_k = expert_ids.shape[1]
    capacity = 4 * tok_rows * top_k // (3 * n_expert)
    slot_count = n_expert * capacity
    gate_w = w_gate[0]
    up_w = w_up[0]
    down_w = w_down[0]
    flat_ids = expert_ids.reshape(-1)
    onehot = (flat_ids[:, None] == jnp.arange(n_expert, dtype=jnp.int32)[None, :]).astype(jnp.int32)
    before = jnp.cumsum(onehot, axis=0) - onehot
    rank_in = jnp.sum(before * onehot, axis=1)
    counts = jnp.sum(onehot, axis=0)
    slot_of = flat_ids * capacity + rank_in
    owner = jnp.arange(flat_ids.shape[0], dtype=jnp.int32) // top_k
    slot_token = jnp.zeros((slot_count,), jnp.int32).at[slot_of].set(owner)
    gate_values = gate_fixed.reshape(-1).astype(jnp.float32) / 65536.0
    slot_gate = jnp.zeros((slot_count,), jnp.float32).at[slot_of].set(gate_values)
    outgoing = jnp.where(
        (slot_gate > 0.0)[:, None], tokens[slot_token], jnp.zeros((), tokens.dtype)
    )
    received, arrived = (
        lax.all_to_all(outgoing, "expert", split_axis=0, concat_axis=0, tiled=True),
        lax.all_to_all(counts, "expert", split_axis=0, concat_axis=0, tiled=True),
    )

    def run_rows(row_fn, inputs):
        return row_fn(*inputs)

    def fold_rows(left, right):
        return contract(left, right)

    expert_out, gate_pre, up_pre, hidden = run_rows(
        partial(forward_rows, gate_w, up_w, down_w), (received,)
    )
    returned = lax.all_to_all(expert_out, "expert", split_axis=0, concat_axis=0, tiled=True)
    mixed_rows = returned[slot_of].astype(jnp.float32).reshape(tok_rows, top_k, width)
    mixed = jnp.sum(mixed_rows * gate_values.reshape(tok_rows, top_k)[:, :, None], axis=1).astype(
        jnp.bfloat16
    )
    dy_out = (cotangent[slot_token].astype(jnp.float32) * slot_gate[:, None]).astype(jnp.bfloat16)
    dy_in = lax.all_to_all(dy_out, "expert", split_axis=0, concat_axis=0, tiled=True)
    d_rows, d_gate, d_up = run_rows(
        partial(backward_rows, gate_w, up_w, down_w), (dy_in, gate_pre, up_pre)
    )
    back_rows = lax.all_to_all(d_rows, "expert", split_axis=0, concat_axis=0, tiled=True)
    token_grad = jnp.sum(
        back_rows[slot_of].astype(jnp.float32).reshape(tok_rows, top_k, width), axis=1
    ).astype(jnp.bfloat16)
    grad_gate, grad_up, grad_down = (
        lax.psum_scatter(
            fold_rows(received, d_gate).astype(jnp.bfloat16), "dp", scatter_dimension=0, tiled=True
        ).astype(jnp.float32),
        lax.psum_scatter(
            fold_rows(received, d_up).astype(jnp.bfloat16), "dp", scatter_dimension=0, tiled=True
        ).astype(jnp.float32),
        lax.psum_scatter(
            fold_rows(hidden, dy_in).astype(jnp.bfloat16), "dp", scatter_dimension=1, tiled=True
        ).astype(jnp.float32),
    )
    return (mixed, token_grad, grad_gate[None], grad_up[None], grad_down[None])


BF16, F32 = jnp.bfloat16, jnp.float32
VMEM = pl.BlockSpec(memory_space=pltpu.VMEM)
SMEM = pl.BlockSpec(memory_space=pltpu.SMEM)
PIECES = ((1, 0), (3, 0), (2, 1), (3, 1), (0, 0), (2, 0), (0, 1), (1, 1))


def tie(*values):
    return lax.optimization_barrier(values)


def nt(left, right):
    return lax.dot_general(left, right, (((1,), (1,)), ((), ())), preferred_element_type=F32)


def nn(left, right):
    return lax.dot_general(left, right, (((1,), (0,)), ((), ())), preferred_element_type=F32)


def tn(left, right):
    return lax.dot_general(left, right, (((0,), (0,)), ((), ())), preferred_element_type=F32)


def call(name, kernel, outs, ins, scratch=(), smem=0, flops=1):
    return list(pl.pallas_call(
        kernel,
        name=name,
        out_shape=[jax.ShapeDtypeStruct(shape, dtype) for shape, dtype in outs],
        in_specs=[SMEM] * smem + [VMEM] * (len(ins) - smem),
        out_specs=[VMEM] * len(outs),
        scratch_shapes=[pltpu.VMEM(shape, dtype) for shape, dtype in scratch],
        compiler_params=pltpu.CompilerParams(vmem_limit_bytes=16 * 1024 * 1024),
        cost_estimate=pl.CostEstimate(flops=flops, bytes_accessed=1, transcendentals=0),
    )(*ins))


def pack_kernel(ids, gates, cot, out):
    n, width = cot.shape
    column = lax.broadcasted_iota(jnp.int32, (n, 128), 1)
    extra = jnp.zeros((n, 128), jnp.int32)
    for at in range(ids.shape[1]):
        expert, gate = ids[:, at : at + 1], gates[:, at : at + 1]
        extra += jnp.where(column == expert, gate >> 8, 0)
        extra += jnp.where(column == expert + 8, gate & 255, 0)
    out[:, :width] = cot[...]
    out[:, width:] = extra.astype(F32).astype(BF16)


def gate_column(expert, extra):
    column = lax.broadcasted_iota(jnp.int32, extra.shape, 1)
    scale = jnp.where(column == expert, 256.0, jnp.where(column == expert + 8, 1.0, 0.0))
    return jnp.sum(extra.astype(F32) * scale, axis=1, keepdims=True) / 65536.0


def forward_kernel(offs, *refs):
    parts, (gate, up, hid, fac_g, fac_u, rows_s, rows_k, rows) = refs[:-8], refs[-8:]
    size = rows.shape[1] // 8
    stack(parts, rows)
    gate_pre = nt(rows[...], gate[...])
    up_pre = nt(rows[...], up[...])
    sigma = jax.nn.sigmoid(gate_pre)
    activ = gate_pre * sigma
    hid[...] = (activ * up_pre).astype(BF16)
    fac_g[...] = up_pre * (sigma * (1.0 + gate_pre * (1.0 - sigma)))
    fac_u[...] = activ
    for at in range(8):
        here = pl.ds(pl.multiple_of(offs[at], size), size)
        (rows_s if at < 4 else rows_k)[:, pl.ds(at % 4 * size, size)] = rows[:, here]


def stack(parts, whole):
    at = 0
    for part in parts:
        whole[at : at + part.shape[0], :] = part[...]
        at += part.shape[0]


def backward_kernel(offs, hid, fac_g, fac_u, down, *refs):
    parts, (out_m, out_o, d_gate, d_up, dy_s, dy_k, held, dy) = refs[:-8], refs[-8:]
    n, width = out_m.shape
    size = width // 8
    stack(parts, held)
    out = nn(hid[...], down[...])
    for at, result in enumerate((out_m, out_o)):
        part = slice(at * n, (at + 1) * n)
        gate = gate_column(offs[8], held[part, width:])
        dy[part, :] = (held[part, :width].astype(F32) * gate).astype(BF16)
        result[...] = (out[part] * gate).astype(BF16)
    d_hid = nt(dy[...], down[...])
    d_gate[...] = (d_hid * fac_g[...]).astype(BF16)
    d_up[...] = (d_hid * fac_u[...]).astype(BF16)
    for at in range(8):
        here = pl.ds(pl.multiple_of(offs[at], size), size)
        (dy_s if at < 4 else dy_k)[:, pl.ds(at % 4 * size, size)] = dy[:, here]


def split_kernel(offs, whole, part_s, part_k):
    width = 2 * part_k.shape[1]
    size = width // 8
    for at in range(8):
        here = pl.ds(pl.multiple_of(offs[at], size), size)
        (part_s if at < 4 else part_k)[:, pl.ds(at % 4 * size, size)] = whole[:, here]
    part_s[:, width // 2 :] = whole[:, width:]


def ahead_kernel(*refs):
    hids, dys, (total, left, right) = refs[:3], refs[3:6], refs[6:]
    stack(hids, left)
    stack(dys, right)
    total[...] = tn(left[...], right[...])


def early_kernel(offs, ahead, hid, *refs):
    parts, (out_a, out_b, dy, gates, held) = refs[:-5], refs[-5:]
    stack(parts, held)
    half = dy.shape[1]
    gate = gate_column(offs[8], held[:, half:])
    gates[...] = jnp.broadcast_to(gate, gates.shape)
    dy[...] = (held[:, :half].astype(F32) * gate).astype(BF16)
    out_a[0, :, :] = (ahead[:, : half // 2] + tn(hid[...], dy[:, : half // 2])).astype(BF16)
    out_b[0, :, :] = (ahead[:, half // 2 :] + tn(hid[...], dy[:, half // 2 :])).astype(BF16)


def out_kernel(hid, down, gates, out_m, out_o):
    n = out_m.shape[0]
    out = nn(hid[...], down[...]) * gates[:, :1]
    out_m[...] = out[:n].astype(BF16)
    out_o[...] = out[n:].astype(BF16)


def sum_kernel(spec, *refs):
    *parts, out = refs
    total, at = 0.0, 0
    for count, low in spec:
        if count == 1:
            term = parts[at][low : low + out.shape[0], :]
        else:
            term = jnp.concatenate([part[...] for part in parts[at : at + count]], axis=0)
        total = total + term.astype(F32)
        at += count
    out[...] = total.astype(BF16)


def last_kernel(offs, gates, fac_g, fac_u, down, dy_s, *refs):
    parts, (d_gate, d_up, dy_k, dy) = refs[:-4], refs[-4:]
    size = down.shape[1] // 8
    stack(parts, dy_k)
    dy_k[...] = (dy_k[...].astype(F32) * gates[:, :1]).astype(BF16)
    for at in range(8):
        here = pl.ds(pl.multiple_of(offs[at], size), size)
        dy[:, here] = (dy_s if at < 4 else dy_k)[:, pl.ds(at % 4 * size, size)]
    d_hid = nt(dy[...], down[...])
    d_gate[...] = (d_hid * fac_g[...]).astype(BF16)
    d_up[...] = (d_hid * fac_u[...]).astype(BF16)


def grads_kernel(groups, *refs):
    ins, (out_a, out_b, left, right) = refs[:-4], refs[-4:]
    half = right.shape[1] // 2
    held = None
    for at, (first, second) in enumerate(groups):
        stack(ins[4 * first : 4 * first + 4], left)
        if second != held:
            stack(ins[4 * second : 4 * second + 4], right)
            held = second
        out_a[at, :, :] = tn(left[...], right[:, :half]).astype(BF16)
        out_b[at, :, :] = tn(left[...], right[:, half:]).astype(BF16)


def cross_kernel(came_a, came_b, down_a, down_b, own_a, own_b, far_a, far_b, near_a, near_b):
    cut = far_a.shape[2]
    for came, down, own, far, near in (
        (came_a, down_a, own_a, far_a, near_a),
        (came_b, down_b, own_b, far_b, near_b),
    ):
        for at in range(3):
            both = (down[0, :, :] if at == 2 else came[at, :, :]).astype(F32) + own[at, :, :].astype(F32)
            near[at, :, :] = both[:, :cut]
            far[at, :, :] = both[:, cut:].astype(BF16)


def finish_kernel(near_a, near_b, last_a, last_b, *outs):
    cut = near_a.shape[2]
    for at, out in enumerate(outs):
        out[:, :cut] = near_a[at, :, :] + last_a[at, :, :].astype(F32)
        out[:, cut:] = near_b[at, :, :] + last_b[at, :, :].astype(F32)


def rows_kernel(*refs):
    d_gate, d_up, gate, up, mine, *others = refs
    n = mine.shape[0]
    size = others[0].shape[0]
    both = nn(d_gate[...], gate[...]) + nn(d_up[...], up[...])
    mine[...] = both[:n].astype(BF16)
    for at, other in enumerate(others):
        other[...] = both[n + at * size : n + (at + 1) * size].astype(BF16)


def ring_order(count):
    return [0] + list(range(1, count, 2)) + [at for at in range(count - 1, 1, -1) if at % 2 == 0]


def step(value, n_expert):
    order = ring_order(n_expert // 2)
    follow = {at: order[(spot + 1) % len(order)] for spot, at in enumerate(order)}
    return lax.ppermute(value, "expert", [(2 * at + core, 2 * follow[at] + core) for at in order for core in range(2)])


def swap(value, n_expert):
    return lax.ppermute(value, "expert", [(at, at ^ 1) for at in range(n_expert)])


def flip(value, mask):
    return lax.ppermute(value, "dp", [(at, at ^ mask) for at in range(4)])


def add(*values):
    return sum(value.astype(F32) for value in values)


class Order:
    def __init__(self, start):
        self.last = start

    def point(self, *values):
        *values, self.last = lax.optimization_barrier((*values, self.last))
        return values

    def after(self, value):
        return lax.optimization_barrier((value, self.last))[0]


def dense_shards(tokens, cotangent, expert_ids, gate_fixed, w_gate, w_up, w_down):
    n_expert = lax.axis_size("expert")
    n, width = tokens.shape
    ff = w_gate.shape[2]
    half, cut = width // 2, width // 8

    def ring(value, name):
        with jax.named_scope(name):
            return step(order.after(value), n_expert)

    def twin(value, name):
        with jax.named_scope(name):
            return swap(order.after(value), n_expert)

    def flips(pair, masks, name):
        with jax.named_scope(name):
            return [flip(order.after(value), mask) for value, mask in zip(pair, masks)]

    def launch(name, kernel, outs, ins, scratch=(), smem=0, flops=1):
        return call(name, kernel, outs, [*ins[:smem], order.after(ins[smem]), *ins[smem + 1 :]], scratch, smem, flops)

    gate_w, up_w, down_w = w_gate[0].T, w_up[0].T, w_down[0]
    me = lax.axis_index("dp")
    offs = [((me ^ rel) * 2 + part) * (width // 8) for rel, part in PIECES]
    offs = jnp.stack([*offs, lax.axis_index("expert")]).astype(jnp.int32)

    def forward(slot, *parts):
        pair = 2 * n
        return launch(
            f"forward_{slot}",
            forward_kernel,
            [((pair, ff), BF16), ((pair, ff), F32), ((pair, ff), F32), ((pair, half), BF16), ((pair, half), BF16)],
            [offs, *parts, gate_w, up_w],
            [((pair, width), BF16)],
            smem=1,
        )

    def backward(slot, ahead, *parts):
        pair = 2 * n
        return launch(
            f"backward_{slot}",
            backward_kernel,
            [((n, width), BF16)] * 2 + [((pair, ff), BF16)] * 2 + [((pair, half), BF16)] * 2,
            [offs, *ahead[:3], down_w, *parts],
            [((pair, width + 128), BF16), ((pair, width), BF16)],
            smem=1,
        )

    def grads(name, groups, *lists):
        return launch(
            name,
            partial(grads_kernel, groups),
            [((len(groups), ff, half // 2), BF16)] * 2,
            [part for parts in lists for part in parts],
            [((8 * n, ff), BF16), ((8 * n, half), BF16)],
        )

    def row_grads(name, slot, cuts=1):
        return launch(
            name,
            rows_kernel,
            [((n, width), BF16)] + [((n // cuts, width), BF16)] * cuts,
            [d_gates[slot], d_ups[slot], gate_w, up_w],
        )

    def pick(value, which):
        return value[which * (n // 2) : (which + 1) * (n // 2)]

    def kept(mine, other, which=None):
        return add(mine, other) if which is None else add(pick(mine, which), pick(other, which))

    def total(near, last, at):
        return jnp.concatenate([add(part[at], more[at]) for part, more in zip(near, last)], axis=1)

    def whole(part_a, part_b, mine, other):
        return jnp.concatenate(
            [add(part_a, kept(mine, other, 0)), add(part_b, kept(mine, other, 1))], axis=0
        ).astype(BF16)

    def twins(value, name):
        return [twin(pick(value, at), f"{name}_{at}") for at in range(2)]

    def early(*parts):
        return launch(
            "early",
            early_kernel,
            [((1, ff, half // 2), BF16)] * 2 + [((2 * n, half), BF16), ((2 * n, 128), F32)],
            [offs, ahead, f3[0], *parts],
            [((2 * n, half + 128), BF16)],
            smem=1,
        )

    def outputs(name, hid, gates):
        return launch(name, out_kernel, [((n, width), BF16)] * 2, [hid, down_w, gates])

    def backward_last(gates, dy_s, *parts):
        return launch(
            "backward_3",
            last_kernel,
            [((2 * n, ff), BF16)] * 2 + [((2 * n, half), BF16)],
            [offs, gates, *f3[1:3], down_w, dy_s, *parts],
            [((2 * n, width), BF16)],
            smem=1,
        )

    def sums(name, *terms, rows=n, low=0):
        terms = [term if isinstance(term, list) else [term] for term in terms]
        spec = tuple((len(term), low if term[0].shape[0] > rows else 0) for term in terms)
        ins = [part for term in terms for part in term]
        return launch(name, partial(sum_kernel, spec), [((rows, width), BF16)], ins)[0]

    order = Order(jnp.zeros((8, 128), F32))
    t0 = tokens
    t1, p0 = ring(t0, "t1"), twin(t0, "p0")
    c0 = launch("pack", pack_kernel, [((n, width + 128), BF16)], [expert_ids, gate_fixed, cotangent])[0]
    c1, q0 = ring(c0, "c1"), twin(c0, "q0")
    (t1,) = order.point(t1)
    t2, p1 = ring(t1, "t2"), twin(t1, "p1")
    c1, p0, p1 = order.point(c1, p0, p1)
    c2, q1 = ring(c1, "c2"), twin(c1, "q1")
    f0 = forward(0, t0, p0)
    f1 = forward(1, t1, p1)
    t2, f0[0], f1[0] = order.point(t2, f0[0], f1[0])
    t3, p2 = ring(t2, "t3"), twin(t2, "p2")
    b0 = backward(0, f0, c0, q0)
    b1 = backward(1, f1, c1, q1)
    o1 = twin(b1[1], "o1")
    c2, p2, b0[0], b1[0] = order.point(c2, p2, b0[0], b1[0])
    c2s, c2k = launch("split", split_kernel, [((n, half + 128), BF16), ((n, half), BF16)], [offs, c2], smem=1)
    c3s = ring(c2s, "c3s")
    q2 = twins(c2, "q2")
    f2 = forward(2, t2, p2)
    b2 = backward(2, f2, c2, *q2)
    o2 = twin(b2[1], "o2")
    ahead = launch(
        "ahead",
        ahead_kernel,
        [((ff, half), F32)],
        [f0[0], f1[0], f2[0], b0[4], b1[4], b2[4]],
        [((6 * n, ff), BF16), ((6 * n, half), BF16)],
    )[0]
    t3, o1, ahead, f2[0], b2[0] = order.point(t3, o1, ahead, f2[0], b2[0])
    c3k = ring(c2k, "c3k")
    p3 = twins(t3, "p3")
    f3 = forward(3, t3, *p3)
    c3s, o2, *f3 = order.point(c3s, o2, *f3)
    m = ring(sums("add_m1", b1[0], o1), "m1")
    q3s = twins(c3s, "q3s")
    hids, facs_g, facs_u, rows_s, rows_k = ([f[at] for f in (f0, f1, f2, f3)] for at in range(5))
    *sent, dy3, gates3 = early(c3s, *q3s)
    dy3, *sent = order.point(dy3, *sent)
    down_came = flips(sent, (1, 2), "d1")
    out3 = outputs("out_3", f3[0], gates3)
    (c3k,) = order.point(c3k)
    q3k = twins(c3k, "q3k")
    b3 = backward_last(gates3, dy3, c3k, *q3k)
    b3 = [*out3, *b3[:2], dy3, b3[2]]
    outs_m, outs_o, d_gates, d_ups, dys_s, dys_k = ([b[at] for b in (b0, b1, b2, b3)] for at in range(6))
    sent = grads("both_s", ((0, 2), (1, 2)), d_gates, d_ups, rows_s)
    d_gates[1], *sent = order.point(d_gates[1], *sent)
    m1, r1 = row_grads("rows_1", 1)
    m, d_gates[2], r1 = order.point(m, d_gates[2], r1)
    m = ring(sums("add_m2", m, outs_m[2], o2), "m2")
    r1, o3 = twin(r1, "r1"), twin(outs_o[3], "o3")
    r1, o3, d_gates[0] = order.point(r1, o3, d_gates[0])
    m2, r2 = row_grads("rows_2", 2)
    r2, d_gates[0], *down_came = order.point(r2, d_gates[0], *down_came)
    both_came = flips(sent, (1, 2), "gu1")
    g = ring(sums("add_g1", m1, r1), "ga1")
    o0 = twin(outs_o[0], "o0")
    m3, r3 = row_grads("rows_3", 3)
    m0, r0 = row_grads("rows_0", 0)
    own = grads("kept_k", ((0, 2), (1, 2), (3, 4)), d_gates, d_ups, rows_k, hids, dys_k)
    m, o0, m3, r3, m0, r0, *own = order.point(m, o0, m3, r3, m0, r0, *own)
    m = ring(sums("add_m3", m, outs_m[3], o3), "m3")
    r2 = twin(r2, "r2")
    g, r2 = order.point(g, r2)
    g = ring(sums("add_g2", g, m2, r2), "ga2")
    r3 = twin(r3, "r3")
    both_came[0], both_came[1], m = order.point(*both_came, m)
    *far, near_a, near_b = launch(
        "cross",
        cross_kernel,
        [((3, ff, cut), BF16)] * 2 + [((3, ff, cut), F32)] * 2,
        [*both_came, *down_came, *own],
    )
    far = order.point(*far)
    last = flips(far, (2, 1), "last")
    g, r3 = order.point(g, r3)
    g = ring(add(g, kept(m3, r3)).astype(BF16), "ga3")
    r0 = twin(r0, "r0")
    mixed = sums("add_m0", m, outs_m[0], o0)
    g, r0, mixed = order.point(g, r0, mixed)
    token_grad = add(g, kept(m0, r0)).astype(BF16)
    token_grad, *last = order.point(token_grad, *last)
    grad_gate, grad_up, grad_down = launch(
        "finish", finish_kernel, [((ff, 2 * cut), F32)] * 3, [near_a, near_b, *last]
    )
    return (mixed, token_grad, grad_gate.T[None], grad_up.T[None], grad_down[None])


def shards(tokens, cotangent, expert_ids, gate_fixed, w_gate, w_up, w_down):
    n_expert = lax.axis_size("expert")
    rows, width = tokens.shape
    capacity = 4 * rows * expert_ids.shape[1] // (3 * n_expert)
    dense = capacity >= rows and n_expert == 8 and lax.axis_size("dp") == 4 and rows == 128 and width % 2048 == 0
    run = dense_shards if dense else slot_shards
    return run(tokens, cotangent, expert_ids, gate_fixed, w_gate, w_up, w_down)


def solution(mesh):
    in_specs = (
        P(("dp", "expert"), None),
        P(("dp", "expert"), None),
        P(("dp", "expert"), None),
        P(("dp", "expert"), None),
        P("expert", None, None),
        P("expert", None, None),
        P("expert", None, None),
    )
    out_specs = (
        P(("dp", "expert"), None),
        P(("dp", "expert"), None),
        P("expert", "dp", None),
        P("expert", "dp", None),
        P("expert", None, "dp"),
    )
    return jax.shard_map(shards, mesh=mesh, in_specs=in_specs, out_specs=out_specs, check_vma=False)
```

```python
from functools import partial

import jax
import jax.numpy as jnp
from jax import lax
from jax.experimental import pallas as pl
from jax.experimental.pallas import tpu as pltpu
from jax.sharding import PartitionSpec as P


def contract(left, right):
    return lax.dot_general(
        left, right, (((0,), (0,)), ((), ())), preferred_element_type=jnp.float32
    )


def trans_dot(left, right):
    return lax.dot_general(
        left, right, (((1,), (1,)), ((), ())), preferred_element_type=jnp.float32
    )


def forward_rows(gate_w, up_w, down_w, rows_in):
    gate_pre = jnp.dot(rows_in, gate_w, preferred_element_type=jnp.float32)
    up_pre = jnp.dot(rows_in, up_w, preferred_element_type=jnp.float32)
    hidden = (gate_pre * jax.nn.sigmoid(gate_pre) * up_pre).astype(jnp.bfloat16)
    expert_out = jnp.dot(hidden, down_w, preferred_element_type=jnp.float32).astype(jnp.bfloat16)
    return (expert_out, gate_pre, up_pre, hidden)


def backward_rows(gate_w, up_w, down_w, dy_rows, gate_pre, up_pre):
    sigma = jax.nn.sigmoid(gate_pre)
    activ = gate_pre * sigma
    d_hidden = trans_dot(dy_rows, down_w)
    d_gate = (d_hidden * up_pre * (sigma * (1.0 + gate_pre * (1.0 - sigma)))).astype(jnp.bfloat16)
    d_up = (d_hidden * activ).astype(jnp.bfloat16)
    d_rows = (trans_dot(d_gate, gate_w) + trans_dot(d_up, up_w)).astype(jnp.bfloat16)
    return (d_rows, d_gate, d_up)


def slot_shards(tokens, cotangent, expert_ids, gate_fixed, w_gate, w_up, w_down):
    n_expert = lax.axis_size("expert")
    tok_rows = tokens.shape[0]
    width = tokens.shape[1]
    top_k = expert_ids.shape[1]
    capacity = 4 * tok_rows * top_k // (3 * n_expert)
    slot_count = n_expert * capacity
    gate_w = w_gate[0]
    up_w = w_up[0]
    down_w = w_down[0]
    flat_ids = expert_ids.reshape(-1)
    onehot = (flat_ids[:, None] == jnp.arange(n_expert, dtype=jnp.int32)[None, :]).astype(jnp.int32)
    before = jnp.cumsum(onehot, axis=0) - onehot
    rank_in = jnp.sum(before * onehot, axis=1)
    counts = jnp.sum(onehot, axis=0)
    slot_of = flat_ids * capacity + rank_in
    owner = jnp.arange(flat_ids.shape[0], dtype=jnp.int32) // top_k
    slot_token = jnp.zeros((slot_count,), jnp.int32).at[slot_of].set(owner)
    gate_values = gate_fixed.reshape(-1).astype(jnp.float32) / 65536.0
    slot_gate = jnp.zeros((slot_count,), jnp.float32).at[slot_of].set(gate_values)
    outgoing = jnp.where(
        (slot_gate > 0.0)[:, None], tokens[slot_token], jnp.zeros((), tokens.dtype)
    )
    received, arrived = (
        lax.all_to_all(outgoing, "expert", split_axis=0, concat_axis=0, tiled=True),
        lax.all_to_all(counts, "expert", split_axis=0, concat_axis=0, tiled=True),
    )

    def run_rows(row_fn, inputs):
        return row_fn(*inputs)

    def fold_rows(left, right):
        return contract(left, right)

    expert_out, gate_pre, up_pre, hidden = run_rows(
        partial(forward_rows, gate_w, up_w, down_w), (received,)
    )
    returned = lax.all_to_all(expert_out, "expert", split_axis=0, concat_axis=0, tiled=True)
    mixed_rows = returned[slot_of].astype(jnp.float32).reshape(tok_rows, top_k, width)
    mixed = jnp.sum(mixed_rows * gate_values.reshape(tok_rows, top_k)[:, :, None], axis=1).astype(
        jnp.bfloat16
    )
    dy_out = (cotangent[slot_token].astype(jnp.float32) * slot_gate[:, None]).astype(jnp.bfloat16)
    dy_in = lax.all_to_all(dy_out, "expert", split_axis=0, concat_axis=0, tiled=True)
    d_rows, d_gate, d_up = run_rows(
        partial(backward_rows, gate_w, up_w, down_w), (dy_in, gate_pre, up_pre)
    )
    back_rows = lax.all_to_all(d_rows, "expert", split_axis=0, concat_axis=0, tiled=True)
    token_grad = jnp.sum(
        back_rows[slot_of].astype(jnp.float32).reshape(tok_rows, top_k, width), axis=1
    ).astype(jnp.bfloat16)
    grad_gate, grad_up, grad_down = (
        lax.psum_scatter(
            fold_rows(received, d_gate).astype(jnp.bfloat16), "dp", scatter_dimension=0, tiled=True
        ).astype(jnp.float32),
        lax.psum_scatter(
            fold_rows(received, d_up).astype(jnp.bfloat16), "dp", scatter_dimension=0, tiled=True
        ).astype(jnp.float32),
        lax.psum_scatter(
            fold_rows(hidden, dy_in).astype(jnp.bfloat16), "dp", scatter_dimension=1, tiled=True
        ).astype(jnp.float32),
    )
    return (mixed, token_grad, grad_gate[None], grad_up[None], grad_down[None])


BF16, F32 = jnp.bfloat16, jnp.float32
VMEM = pl.BlockSpec(memory_space=pltpu.VMEM)
SMEM = pl.BlockSpec(memory_space=pltpu.SMEM)
PIECES = ((1, 0), (3, 0), (2, 1), (3, 1), (0, 0), (2, 0), (0, 1), (1, 1))


def tie(*values):
    return lax.optimization_barrier(values)


def nt(left, right):
    return lax.dot_general(left, right, (((1,), (1,)), ((), ())), preferred_element_type=F32)


def nn(left, right):
    return lax.dot_general(left, right, (((1,), (0,)), ((), ())), preferred_element_type=F32)


def tn(left, right):
    return lax.dot_general(left, right, (((0,), (0,)), ((), ())), preferred_element_type=F32)


def call(name, kernel, outs, ins, scratch=(), smem=0, flops=1):
    return list(pl.pallas_call(
        kernel,
        name=name,
        out_shape=[jax.ShapeDtypeStruct(shape, dtype) for shape, dtype in outs],
        in_specs=[SMEM] * smem + [VMEM] * (len(ins) - smem),
        out_specs=[VMEM] * len(outs),
        scratch_shapes=[pltpu.VMEM(shape, dtype) for shape, dtype in scratch],
        compiler_params=pltpu.CompilerParams(vmem_limit_bytes=16 * 1024 * 1024),
        cost_estimate=pl.CostEstimate(flops=flops, bytes_accessed=1, transcendentals=0),
    )(*ins))


def pack_kernel(ids, gates, cot, out):
    n, width = cot.shape
    column = lax.broadcasted_iota(jnp.int32, (n, 128), 1)
    extra = jnp.zeros((n, 128), jnp.int32)
    for at in range(ids.shape[1]):
        expert, gate = ids[:, at : at + 1], gates[:, at : at + 1]
        extra += jnp.where(column == expert, gate >> 8, 0)
        extra += jnp.where(column == expert + 8, gate & 255, 0)
    out[:, :width] = cot[...]
    out[:, width:] = extra.astype(F32).astype(BF16)


def gate_column(expert, extra):
    column = lax.broadcasted_iota(jnp.int32, extra.shape, 1)
    scale = jnp.where(column == expert, 256.0, jnp.where(column == expert + 8, 1.0, 0.0))
    return jnp.sum(extra.astype(F32) * scale, axis=1, keepdims=True) / 65536.0


def forward_kernel(offs, *refs):
    parts, (gate, up, hid, fac_g, fac_u, rows_s, rows_k, rows) = refs[:-8], refs[-8:]
    size = rows.shape[1] // 8
    stack(parts, rows)
    gate_pre = nt(rows[...], gate[...])
    up_pre = nt(rows[...], up[...])
    sigma = jax.nn.sigmoid(gate_pre)
    activ = gate_pre * sigma
    hid[...] = (activ * up_pre).astype(BF16)
    fac_g[...] = up_pre * (sigma * (1.0 + gate_pre * (1.0 - sigma)))
    fac_u[...] = activ
    for at in range(8):
        here = pl.ds(pl.multiple_of(offs[at], size), size)
        (rows_s if at < 4 else rows_k)[:, pl.ds(at % 4 * size, size)] = rows[:, here]


def stack(parts, whole):
    at = 0
    for part in parts:
        whole[at : at + part.shape[0], :] = part[...]
        at += part.shape[0]


def backward_kernel(offs, hid, fac_g, fac_u, down, *refs):
    parts, (out_m, out_o, d_gate, d_up, dy_s, dy_k, held, dy) = refs[:-8], refs[-8:]
    n, width = out_m.shape
    size = width // 8
    stack(parts, held)
    out = nn(hid[...], down[...])
    for at, result in enumerate((out_m, out_o)):
        part = slice(at * n, (at + 1) * n)
        gate = gate_column(offs[8], held[part, width:])
        dy[part, :] = (held[part, :width].astype(F32) * gate).astype(BF16)
        result[...] = (out[part] * gate).astype(BF16)
    d_hid = nt(dy[...], down[...])
    d_gate[...] = (d_hid * fac_g[...]).astype(BF16)
    d_up[...] = (d_hid * fac_u[...]).astype(BF16)
    for at in range(8):
        here = pl.ds(pl.multiple_of(offs[at], size), size)
        (dy_s if at < 4 else dy_k)[:, pl.ds(at % 4 * size, size)] = dy[:, here]


def split_kernel(offs, whole, part_s, part_k):
    width = 2 * part_k.shape[1]
    size = width // 8
    for at in range(8):
        here = pl.ds(pl.multiple_of(offs[at], size), size)
        (part_s if at < 4 else part_k)[:, pl.ds(at % 4 * size, size)] = whole[:, here]
    part_s[:, width // 2 :] = whole[:, width:]


def ahead_kernel(*refs):
    hids, dys, (total, left, right) = refs[:3], refs[3:6], refs[6:]
    stack(hids, left)
    stack(dys, right)
    total[...] = tn(left[...], right[...])


def early_kernel(offs, ahead, hid, *refs):
    parts, (out_a, out_b, dy, gates, held) = refs[:-5], refs[-5:]
    stack(parts, held)
    half = dy.shape[1]
    gate = gate_column(offs[8], held[:, half:])
    gates[...] = jnp.broadcast_to(gate, gates.shape)
    dy[...] = (held[:, :half].astype(F32) * gate).astype(BF16)
    out_a[0, :, :] = (ahead[:, : half // 2] + tn(hid[...], dy[:, : half // 2])).astype(BF16)
    out_b[0, :, :] = (ahead[:, half // 2 :] + tn(hid[...], dy[:, half // 2 :])).astype(BF16)


def out_kernel(hid, down, gates, out_m, out_o):
    n = out_m.shape[0]
    out = nn(hid[...], down[...]) * gates[:, :1]
    out_m[...] = out[:n].astype(BF16)
    out_o[...] = out[n:].astype(BF16)


def sum_kernel(spec, *refs):
    *parts, out = refs
    total, at = 0.0, 0
    for count, low in spec:
        if count == 1:
            term = parts[at][low : low + out.shape[0], :]
        else:
            term = jnp.concatenate([part[...] for part in parts[at : at + count]], axis=0)
        total = total + term.astype(F32)
        at += count
    out[...] = total.astype(BF16)


def last_kernel(offs, gates, fac_g, fac_u, down, dy_s, *refs):
    parts, (d_gate, d_up, dy_k, dy) = refs[:-4], refs[-4:]
    size = down.shape[1] // 8
    stack(parts, dy_k)
    dy_k[...] = (dy_k[...].astype(F32) * gates[:, :1]).astype(BF16)
    for at in range(8):
        here = pl.ds(pl.multiple_of(offs[at], size), size)
        dy[:, here] = (dy_s if at < 4 else dy_k)[:, pl.ds(at % 4 * size, size)]
    d_hid = nt(dy[...], down[...])
    d_gate[...] = (d_hid * fac_g[...]).astype(BF16)
    d_up[...] = (d_hid * fac_u[...]).astype(BF16)


def grads_kernel(groups, *refs):
    ins, (out_a, out_b, left, right) = refs[:-4], refs[-4:]
    half = right.shape[1] // 2
    held = None
    for at, (first, second) in enumerate(groups):
        stack(ins[4 * first : 4 * first + 4], left)
        if second != held:
            stack(ins[4 * second : 4 * second + 4], right)
            held = second
        out_a[at, :, :] = tn(left[...], right[:, :half]).astype(BF16)
        out_b[at, :, :] = tn(left[...], right[:, half:]).astype(BF16)


def cross_kernel(near, came_a, came_b, down_a, down_b, own_a, own_b, *outs):
    cut = outs[0].shape[2]
    part = slice(0, cut) if near else slice(cut, 2 * cut)
    for came, down, own, out in ((came_a, down_a, own_a, outs[0]), (came_b, down_b, own_b, outs[1])):
        for at in range(3):
            first = down[0, :, part] if at == 2 else came[at, :, part]
            out[at, :, :] = (first.astype(F32) + own[at, :, part].astype(F32)).astype(out.dtype)


def finish_kernel(near_a, near_b, last_a, last_b, *outs):
    cut = near_a.shape[2]
    for at, out in enumerate(outs):
        out[:, :cut] = near_a[at, :, :] + last_a[at, :, :].astype(F32)
        out[:, cut:] = near_b[at, :, :] + last_b[at, :, :].astype(F32)


def rows_kernel(*refs):
    d_gate, d_up, gate, up, mine, *others = refs
    n = mine.shape[0]
    size = others[0].shape[0]
    both = nn(d_gate[...], gate[...]) + nn(d_up[...], up[...])
    mine[...] = both[:n].astype(BF16)
    for at, other in enumerate(others):
        other[...] = both[n + at * size : n + (at + 1) * size].astype(BF16)


def ring_order(count):
    return [0] + list(range(1, count, 2)) + [at for at in range(count - 1, 1, -1) if at % 2 == 0]


def step(value, n_expert):
    order = ring_order(n_expert // 2)
    follow = {at: order[(spot + 1) % len(order)] for spot, at in enumerate(order)}
    return lax.ppermute(value, "expert", [(2 * at + core, 2 * follow[at] + core) for at in order for core in range(2)])


def swap(value, n_expert):
    return lax.ppermute(value, "expert", [(at, at ^ 1) for at in range(n_expert)])


def flip(value, mask):
    return lax.ppermute(value, "dp", [(at, at ^ mask) for at in range(4)])


def add(*values):
    return sum(value.astype(F32) for value in values)


class Order:
    def __init__(self, start):
        self.last = start

    def point(self, *values):
        *values, self.last = lax.optimization_barrier((*values, self.last))
        return values

    def after(self, value):
        return lax.optimization_barrier((value, self.last))[0]


def dense_shards(tokens, cotangent, expert_ids, gate_fixed, w_gate, w_up, w_down):
    n_expert = lax.axis_size("expert")
    n, width = tokens.shape
    ff = w_gate.shape[2]
    half, cut = width // 2, width // 8

    def ring(value, name):
        with jax.named_scope(name):
            return step(order.after(value), n_expert)

    def twin(value, name):
        with jax.named_scope(name):
            return swap(order.after(value), n_expert)

    def flips(pair, masks, name):
        with jax.named_scope(name):
            return [flip(order.after(value), mask) for value, mask in zip(pair, masks)]

    def launch(name, kernel, outs, ins, scratch=(), smem=0, flops=1):
        return call(name, kernel, outs, [*ins[:smem], order.after(ins[smem]), *ins[smem + 1 :]], scratch, smem, flops)

    gate_w, up_w, down_w = w_gate[0].T, w_up[0].T, w_down[0]
    me = lax.axis_index("dp")
    offs = [((me ^ rel) * 2 + part) * (width // 8) for rel, part in PIECES]
    offs = jnp.stack([*offs, lax.axis_index("expert")]).astype(jnp.int32)

    def forward(slot, *parts):
        pair = 2 * n
        return launch(
            f"forward_{slot}",
            forward_kernel,
            [((pair, ff), BF16), ((pair, ff), F32), ((pair, ff), F32), ((pair, half), BF16), ((pair, half), BF16)],
            [offs, *parts, gate_w, up_w],
            [((pair, width), BF16)],
            smem=1,
        )

    def backward(slot, ahead, *parts):
        pair = 2 * n
        return launch(
            f"backward_{slot}",
            backward_kernel,
            [((n, width), BF16)] * 2 + [((pair, ff), BF16)] * 2 + [((pair, half), BF16)] * 2,
            [offs, *ahead[:3], down_w, *parts],
            [((pair, width + 128), BF16), ((pair, width), BF16)],
            smem=1,
        )

    def grads(name, groups, *lists):
        return launch(
            name,
            partial(grads_kernel, groups),
            [((len(groups), ff, half // 2), BF16)] * 2,
            [part for parts in lists for part in parts],
            [((8 * n, ff), BF16), ((8 * n, half), BF16)],
        )

    def row_grads(name, slot, cuts=1):
        return launch(
            name,
            rows_kernel,
            [((n, width), BF16)] + [((n // cuts, width), BF16)] * cuts,
            [d_gates[slot], d_ups[slot], gate_w, up_w],
        )

    def pick(value, which):
        return value[which * (n // 2) : (which + 1) * (n // 2)]

    def kept(mine, other, which=None):
        return add(mine, other) if which is None else add(pick(mine, which), pick(other, which))

    def total(near, last, at):
        return jnp.concatenate([add(part[at], more[at]) for part, more in zip(near, last)], axis=1)

    def whole(part_a, part_b, mine, other):
        return jnp.concatenate(
            [add(part_a, kept(mine, other, 0)), add(part_b, kept(mine, other, 1))], axis=0
        ).astype(BF16)

    def twins(value, name):
        return [twin(pick(value, at), f"{name}_{at}") for at in range(2)]

    def early(*parts):
        return launch(
            "early",
            early_kernel,
            [((1, ff, half // 2), BF16)] * 2 + [((2 * n, half), BF16), ((2 * n, 128), F32)],
            [offs, ahead, f3[0], *parts],
            [((2 * n, half + 128), BF16)],
            smem=1,
        )

    def outputs(name, hid, gates):
        return launch(name, out_kernel, [((n, width), BF16)] * 2, [hid, down_w, gates])

    def backward_last(gates, dy_s, *parts):
        return launch(
            "backward_3",
            last_kernel,
            [((2 * n, ff), BF16)] * 2 + [((2 * n, half), BF16)],
            [offs, gates, *f3[1:3], down_w, dy_s, *parts],
            [((2 * n, width), BF16)],
            smem=1,
        )

    def sums(name, *terms, rows=n, low=0):
        terms = [term if isinstance(term, list) else [term] for term in terms]
        spec = tuple((len(term), low if term[0].shape[0] > rows else 0) for term in terms)
        ins = [part for term in terms for part in term]
        return launch(name, partial(sum_kernel, spec), [((rows, width), BF16)], ins)[0]

    order = Order(jnp.zeros((8, 128), F32))
    t0 = tokens
    t1, p0 = ring(t0, "t1"), twin(t0, "p0")
    c0 = launch("pack", pack_kernel, [((n, width + 128), BF16)], [expert_ids, gate_fixed, cotangent])[0]
    c1, q0 = ring(c0, "c1"), twin(c0, "q0")
    (t1,) = order.point(t1)
    t2, p1 = ring(t1, "t2"), twin(t1, "p1")
    c1, p0, p1 = order.point(c1, p0, p1)
    c2, q1 = ring(c1, "c2"), twin(c1, "q1")
    f0 = forward(0, t0, p0)
    f1 = forward(1, t1, p1)
    t2, f0[0], f1[0] = order.point(t2, f0[0], f1[0])
    t3, p2 = ring(t2, "t3"), twin(t2, "p2")
    b0 = backward(0, f0, c0, q0)
    b1 = backward(1, f1, c1, q1)
    o1 = twin(b1[1], "o1")
    c2, p2, b0[0], b1[0] = order.point(c2, p2, b0[0], b1[0])
    c2s, c2k = launch("split", split_kernel, [((n, half + 128), BF16), ((n, half), BF16)], [offs, c2], smem=1)
    c3s = ring(c2s, "c3s")
    q2 = twins(c2, "q2")
    f2 = forward(2, t2, p2)
    b2 = backward(2, f2, c2, *q2)
    o2 = twin(b2[1], "o2")
    ahead = launch(
        "ahead",
        ahead_kernel,
        [((ff, half), F32)],
        [f0[0], f1[0], f2[0], b0[4], b1[4], b2[4]],
        [((6 * n, ff), BF16), ((6 * n, half), BF16)],
    )[0]
    t3, o1, ahead, f2[0], b2[0] = order.point(t3, o1, ahead, f2[0], b2[0])
    c3k = ring(c2k, "c3k")
    p3 = twins(t3, "p3")
    f3 = forward(3, t3, *p3)
    c3s, o2, *f3 = order.point(c3s, o2, *f3)
    m = ring(sums("add_m1", b1[0], o1), "m1")
    q3s = twins(c3s, "q3s")
    hids, facs_g, facs_u, rows_s, rows_k = ([f[at] for f in (f0, f1, f2, f3)] for at in range(5))
    *sent, dy3, gates3 = early(c3s, *q3s)
    dy3, *sent = order.point(dy3, *sent)
    down_came = flips(sent, (1, 2), "d1")
    out3 = outputs("out_3", f3[0], gates3)
    (c3k,) = order.point(c3k)
    q3k = twins(c3k, "q3k")
    b3 = backward_last(gates3, dy3, c3k, *q3k)
    b3 = [*out3, *b3[:2], dy3, b3[2]]
    outs_m, outs_o, d_gates, d_ups, dys_s, dys_k = ([b[at] for b in (b0, b1, b2, b3)] for at in range(6))
    sent = grads("both_s", ((0, 2), (1, 2)), d_gates, d_ups, rows_s)
    d_gates[1], *sent = order.point(d_gates[1], *sent)
    m1, r1 = row_grads("rows_1", 1)
    m, d_gates[2], r1 = order.point(m, d_gates[2], r1)
    m = ring(sums("add_m2", m, outs_m[2], o2), "m2")
    r1, o3 = twin(r1, "r1"), twin(outs_o[3], "o3")
    r1, o3, d_gates[0] = order.point(r1, o3, d_gates[0])
    m2, r2 = row_grads("rows_2", 2)
    r2, d_gates[0], *down_came = order.point(r2, d_gates[0], *down_came)
    both_came = flips(sent, (1, 2), "gu1")
    g = ring(sums("add_g1", m1, r1), "ga1")
    o0 = twin(outs_o[0], "o0")
    m3, r3 = row_grads("rows_3", 3)
    m0, r0 = row_grads("rows_0", 0)
    own = grads("kept_k", ((0, 2), (1, 2), (3, 4)), d_gates, d_ups, rows_k, hids, dys_k)
    m, o0, m3, r3, m0, r0, *own = order.point(m, o0, m3, r3, m0, r0, *own)
    m = ring(sums("add_m3", m, outs_m[3], o3), "m3")
    r2 = twin(r2, "r2")
    g, r2 = order.point(g, r2)
    g = ring(sums("add_g2", g, m2, r2), "ga2")
    r3 = twin(r3, "r3")
    both_came[0], both_came[1], m = order.point(*both_came, m)
    parts = [*both_came, *down_came, *own]
    far = launch("cross", partial(cross_kernel, False), [((3, ff, cut), BF16)] * 2, parts)
    far = order.point(*far)
    last = flips(far, (2, 1), "last")
    near_a, near_b = launch("settle", partial(cross_kernel, True), [((3, ff, cut), F32)] * 2, parts)
    g, r3 = order.point(g, r3)
    g = ring(add(g, kept(m3, r3)).astype(BF16), "ga3")
    r0 = twin(r0, "r0")
    mixed = sums("add_m0", m, outs_m[0], o0)
    g, r0, mixed, near_a, near_b = order.point(g, r0, mixed, near_a, near_b)
    token_grad = add(g, kept(m0, r0)).astype(BF16)
    token_grad, *last = order.point(token_grad, *last)
    grad_gate, grad_up, grad_down = launch(
        "finish", finish_kernel, [((ff, 2 * cut), F32)] * 3, [near_a, near_b, *last]
    )
    return (mixed, token_grad, grad_gate.T[None], grad_up.T[None], grad_down[None])


def shards(tokens, cotangent, expert_ids, gate_fixed, w_gate, w_up, w_down):
    n_expert = lax.axis_size("expert")
    rows, width = tokens.shape
    capacity = 4 * rows * expert_ids.shape[1] // (3 * n_expert)
    dense = capacity >= rows and n_expert == 8 and lax.axis_size("dp") == 4 and rows == 128 and width % 2048 == 0
    run = dense_shards if dense else slot_shards
    return run(tokens, cotangent, expert_ids, gate_fixed, w_gate, w_up, w_down)


def solution(mesh):
    in_specs = (
        P(("dp", "expert"), None),
        P(("dp", "expert"), None),
        P(("dp", "expert"), None),
        P(("dp", "expert"), None),
        P("expert", None, None),
        P("expert", None, None),
        P("expert", None, None),
    )
    out_specs = (
        P(("dp", "expert"), None),
        P(("dp", "expert"), None),
        P("expert", "dp", None),
        P("expert", "dp", None),
        P("expert", None, "dp"),
    )
    return jax.shard_map(shards, mesh=mesh, in_specs=in_specs, out_specs=out_specs, check_vma=False)
```

```python
from functools import partial

import jax
import jax.numpy as jnp
from jax import lax
from jax.experimental import pallas as pl
from jax.experimental.pallas import tpu as pltpu
from jax.sharding import PartitionSpec as P


def contract(left, right):
    return lax.dot_general(
        left, right, (((0,), (0,)), ((), ())), preferred_element_type=jnp.float32
    )


def trans_dot(left, right):
    return lax.dot_general(
        left, right, (((1,), (1,)), ((), ())), preferred_element_type=jnp.float32
    )


def forward_rows(gate_w, up_w, down_w, rows_in):
    gate_pre = jnp.dot(rows_in, gate_w, preferred_element_type=jnp.float32)
    up_pre = jnp.dot(rows_in, up_w, preferred_element_type=jnp.float32)
    hidden = (gate_pre * jax.nn.sigmoid(gate_pre) * up_pre).astype(jnp.bfloat16)
    expert_out = jnp.dot(hidden, down_w, preferred_element_type=jnp.float32).astype(jnp.bfloat16)
    return (expert_out, gate_pre, up_pre, hidden)


def backward_rows(gate_w, up_w, down_w, dy_rows, gate_pre, up_pre):
    sigma = jax.nn.sigmoid(gate_pre)
    activ = gate_pre * sigma
    d_hidden = trans_dot(dy_rows, down_w)
    d_gate = (d_hidden * up_pre * (sigma * (1.0 + gate_pre * (1.0 - sigma)))).astype(jnp.bfloat16)
    d_up = (d_hidden * activ).astype(jnp.bfloat16)
    d_rows = (trans_dot(d_gate, gate_w) + trans_dot(d_up, up_w)).astype(jnp.bfloat16)
    return (d_rows, d_gate, d_up)


def slot_shards(tokens, cotangent, expert_ids, gate_fixed, w_gate, w_up, w_down):
    n_expert = lax.axis_size("expert")
    tok_rows = tokens.shape[0]
    width = tokens.shape[1]
    top_k = expert_ids.shape[1]
    capacity = 4 * tok_rows * top_k // (3 * n_expert)
    slot_count = n_expert * capacity
    gate_w = w_gate[0]
    up_w = w_up[0]
    down_w = w_down[0]
    flat_ids = expert_ids.reshape(-1)
    onehot = (flat_ids[:, None] == jnp.arange(n_expert, dtype=jnp.int32)[None, :]).astype(jnp.int32)
    before = jnp.cumsum(onehot, axis=0) - onehot
    rank_in = jnp.sum(before * onehot, axis=1)
    counts = jnp.sum(onehot, axis=0)
    slot_of = flat_ids * capacity + rank_in
    owner = jnp.arange(flat_ids.shape[0], dtype=jnp.int32) // top_k
    slot_token = jnp.zeros((slot_count,), jnp.int32).at[slot_of].set(owner)
    gate_values = gate_fixed.reshape(-1).astype(jnp.float32) / 65536.0
    slot_gate = jnp.zeros((slot_count,), jnp.float32).at[slot_of].set(gate_values)
    outgoing = jnp.where(
        (slot_gate > 0.0)[:, None], tokens[slot_token], jnp.zeros((), tokens.dtype)
    )
    received, arrived = (
        lax.all_to_all(outgoing, "expert", split_axis=0, concat_axis=0, tiled=True),
        lax.all_to_all(counts, "expert", split_axis=0, concat_axis=0, tiled=True),
    )

    def run_rows(row_fn, inputs):
        return row_fn(*inputs)

    def fold_rows(left, right):
        return contract(left, right)

    expert_out, gate_pre, up_pre, hidden = run_rows(
        partial(forward_rows, gate_w, up_w, down_w), (received,)
    )
    returned = lax.all_to_all(expert_out, "expert", split_axis=0, concat_axis=0, tiled=True)
    mixed_rows = returned[slot_of].astype(jnp.float32).reshape(tok_rows, top_k, width)
    mixed = jnp.sum(mixed_rows * gate_values.reshape(tok_rows, top_k)[:, :, None], axis=1).astype(
        jnp.bfloat16
    )
    dy_out = (cotangent[slot_token].astype(jnp.float32) * slot_gate[:, None]).astype(jnp.bfloat16)
    dy_in = lax.all_to_all(dy_out, "expert", split_axis=0, concat_axis=0, tiled=True)
    d_rows, d_gate, d_up = run_rows(
        partial(backward_rows, gate_w, up_w, down_w), (dy_in, gate_pre, up_pre)
    )
    back_rows = lax.all_to_all(d_rows, "expert", split_axis=0, concat_axis=0, tiled=True)
    token_grad = jnp.sum(
        back_rows[slot_of].astype(jnp.float32).reshape(tok_rows, top_k, width), axis=1
    ).astype(jnp.bfloat16)
    grad_gate, grad_up, grad_down = (
        lax.psum_scatter(
            fold_rows(received, d_gate).astype(jnp.bfloat16), "dp", scatter_dimension=0, tiled=True
        ).astype(jnp.float32),
        lax.psum_scatter(
            fold_rows(received, d_up).astype(jnp.bfloat16), "dp", scatter_dimension=0, tiled=True
        ).astype(jnp.float32),
        lax.psum_scatter(
            fold_rows(hidden, dy_in).astype(jnp.bfloat16), "dp", scatter_dimension=1, tiled=True
        ).astype(jnp.float32),
    )
    return (mixed, token_grad, grad_gate[None], grad_up[None], grad_down[None])


BF16, F32 = jnp.bfloat16, jnp.float32
VMEM = pl.BlockSpec(memory_space=pltpu.VMEM)
SMEM = pl.BlockSpec(memory_space=pltpu.SMEM)
PIECES = ((1, 0), (3, 0), (2, 1), (3, 1), (0, 0), (2, 0), (0, 1), (1, 1))


def tie(*values):
    return lax.optimization_barrier(values)


def nt(left, right):
    return lax.dot_general(left, right, (((1,), (1,)), ((), ())), preferred_element_type=F32)


def nn(left, right):
    return lax.dot_general(left, right, (((1,), (0,)), ((), ())), preferred_element_type=F32)


def tn(left, right):
    return lax.dot_general(left, right, (((0,), (0,)), ((), ())), preferred_element_type=F32)


def call(name, kernel, outs, ins, scratch=(), smem=0, copies=0):
    return list(pl.pallas_call(
        kernel,
        name=name,
        out_shape=[jax.ShapeDtypeStruct(shape, dtype) for shape, dtype in outs],
        in_specs=[SMEM] * smem + [VMEM] * (len(ins) - smem),
        out_specs=[pl.BlockSpec(memory_space=pl.ANY) if copies else VMEM] * len(outs),
        scratch_shapes=[pltpu.VMEM(shape, dtype) for shape, dtype in scratch]
        + ([pltpu.SemaphoreType.DMA((copies,))] if copies else []),
        compiler_params=pltpu.CompilerParams(vmem_limit_bytes=16 * 1024 * 1024),
        cost_estimate=pl.CostEstimate(flops=1, bytes_accessed=1, transcendentals=0),
    )(*ins))


def pack_kernel(ids, gates, cot, out):
    n, width = cot.shape
    column = lax.broadcasted_iota(jnp.int32, (n, 128), 1)
    extra = jnp.zeros((n, 128), jnp.int32)
    for at in range(ids.shape[1]):
        expert, gate = ids[:, at : at + 1], gates[:, at : at + 1]
        extra += jnp.where(column == expert, gate >> 8, 0)
        extra += jnp.where(column == expert + 8, gate & 255, 0)
    out[:, :width] = cot[...]
    out[:, width:] = extra.astype(F32).astype(BF16)


def gate_column(expert, extra):
    column = lax.broadcasted_iota(jnp.int32, extra.shape, 1)
    scale = jnp.where(column == expert, 256.0, jnp.where(column == expert + 8, 1.0, 0.0))
    return jnp.sum(extra.astype(F32) * scale, axis=1, keepdims=True) / 65536.0


def forward_kernel(offs, *refs):
    parts, (gate, up, hid, fac_g, fac_u, rows_s, rows_k, rows) = refs[:-8], refs[-8:]
    size = rows.shape[1] // 8
    stack(parts, rows)
    gate_pre = nt(rows[...], gate[...])
    up_pre = nt(rows[...], up[...])
    sigma = jax.nn.sigmoid(gate_pre)
    activ = gate_pre * sigma
    hid[...] = (activ * up_pre).astype(BF16)
    fac_g[...] = up_pre * (sigma * (1.0 + gate_pre * (1.0 - sigma)))
    fac_u[...] = activ
    for at in range(8):
        here = pl.ds(pl.multiple_of(offs[at], size), size)
        (rows_s if at < 4 else rows_k)[:, pl.ds(at % 4 * size, size)] = rows[:, here]


def stack(parts, whole):
    at = 0
    for part in parts:
        whole[at : at + part.shape[0], :] = part[...]
        at += part.shape[0]


def backward_kernel(offs, hid, fac_g, fac_u, down, *refs):
    parts, (out_m, out_o, d_gate, d_up, dy_s, dy_k, held, dy) = refs[:-8], refs[-8:]
    n, width = out_m.shape
    size = width // 8
    stack(parts, held)
    out = nn(hid[...], down[...])
    for at, result in enumerate((out_m, out_o)):
        part = slice(at * n, (at + 1) * n)
        gate = gate_column(offs[8], held[part, width:])
        dy[part, :] = (held[part, :width].astype(F32) * gate).astype(BF16)
        result[...] = (out[part] * gate).astype(BF16)
    d_hid = nt(dy[...], down[...])
    d_gate[...] = (d_hid * fac_g[...]).astype(BF16)
    d_up[...] = (d_hid * fac_u[...]).astype(BF16)
    for at in range(8):
        here = pl.ds(pl.multiple_of(offs[at], size), size)
        (dy_s if at < 4 else dy_k)[:, pl.ds(at % 4 * size, size)] = dy[:, here]


def split_kernel(offs, whole, part_s, part_k):
    width = 2 * part_k.shape[1]
    size = width // 8
    for at in range(8):
        here = pl.ds(pl.multiple_of(offs[at], size), size)
        (part_s if at < 4 else part_k)[:, pl.ds(at % 4 * size, size)] = whole[:, here]
    part_s[:, width // 2 :] = whole[:, width:]


def ahead_kernel(*refs):
    hids, dys, (total, left, right) = refs[:3], refs[3:6], refs[6:]
    stack(hids, left)
    stack(dys, right)
    total[...] = tn(left[...], right[...])


def early_kernel(offs, ahead, hid, *refs):
    parts, (out_a, out_b, dy, gates, held) = refs[:-5], refs[-5:]
    stack(parts, held)
    half = dy.shape[1]
    gate = gate_column(offs[8], held[:, half:])
    gates[...] = jnp.broadcast_to(gate, gates.shape)
    dy[...] = (held[:, :half].astype(F32) * gate).astype(BF16)
    out_a[0, :, :] = (ahead[:, : half // 2] + tn(hid[...], dy[:, : half // 2])).astype(BF16)
    out_b[0, :, :] = (ahead[:, half // 2 :] + tn(hid[...], dy[:, half // 2 :])).astype(BF16)


def out_kernel(hid, down, gates, out_m, out_o):
    n = out_m.shape[0]
    out = nn(hid[...], down[...]) * gates[:, :1]
    out_m[...] = out[:n].astype(BF16)
    out_o[...] = out[n:].astype(BF16)


def sum_kernel(spec, *refs):
    *parts, out = refs
    total, at = 0.0, 0
    for count, low in spec:
        if count == 1:
            term = parts[at][low : low + out.shape[0], :]
        else:
            term = jnp.concatenate([part[...] for part in parts[at : at + count]], axis=0)
        total = total + term.astype(F32)
        at += count
    out[...] = total.astype(BF16)


def last_kernel(offs, gates, fac_g, fac_u, down, dy_s, *refs):
    parts, (d_gate, d_up, dy_k, dy) = refs[:-4], refs[-4:]
    size = down.shape[1] // 8
    stack(parts, dy_k)
    dy_k[...] = (dy_k[...].astype(F32) * gates[:, :1]).astype(BF16)
    for at in range(8):
        here = pl.ds(pl.multiple_of(offs[at], size), size)
        dy[:, here] = (dy_s if at < 4 else dy_k)[:, pl.ds(at % 4 * size, size)]
    d_hid = nt(dy[...], down[...])
    d_gate[...] = (d_hid * fac_g[...]).astype(BF16)
    d_up[...] = (d_hid * fac_u[...]).astype(BF16)


def grads_kernel(groups, *refs):
    ins, (out_a, out_b, left, right) = refs[:-4], refs[-4:]
    half = right.shape[1] // 2
    held = None
    for at, (first, second) in enumerate(groups):
        stack(ins[4 * first : 4 * first + 4], left)
        if second != held:
            stack(ins[4 * second : 4 * second + 4], right)
            held = second
        out_a[at, :, :] = tn(left[...], right[:, :half]).astype(BF16)
        out_b[at, :, :] = tn(left[...], right[:, half:]).astype(BF16)


def cross_kernel(near, came_a, came_b, down_a, down_b, own_a, own_b, *outs):
    cut = outs[0].shape[2]
    part = slice(0, cut) if near else slice(cut, 2 * cut)
    for came, down, own, out in ((came_a, down_a, own_a, outs[0]), (came_b, down_b, own_b, outs[1])):
        for at in range(3):
            first = down[0, :, part] if at == 2 else came[at, :, part]
            out[at, :, :] = (first.astype(F32) + own[at, :, part].astype(F32)).astype(out.dtype)


def finish_kernel(near_a, near_b, last_a, last_b, *refs):
    outs, (held, sems) = refs[:-2], refs[-2:]
    cut = near_a.shape[2]
    copies = []
    for at, out in enumerate(outs):
        held[at, :, :cut] = near_a[at, :, :] + last_a[at, :, :].astype(F32)
        held[at, :, cut:] = near_b[at, :, :] + last_b[at, :, :].astype(F32)
        copies.append(pltpu.make_async_copy(held.at[at], out, sems.at[at]))
        copies[-1].start()
    for copy in copies:
        copy.wait()


def rows_kernel(*refs):
    d_gate, d_up, gate, up, mine, *others = refs
    n = mine.shape[0]
    size = others[0].shape[0]
    both = nn(d_gate[...], gate[...]) + nn(d_up[...], up[...])
    mine[...] = both[:n].astype(BF16)
    for at, other in enumerate(others):
        other[...] = both[n + at * size : n + (at + 1) * size].astype(BF16)


def ring_order(count):
    return [0] + list(range(1, count, 2)) + [at for at in range(count - 1, 1, -1) if at % 2 == 0]


def step(value, n_expert):
    order = ring_order(n_expert // 2)
    follow = {at: order[(spot + 1) % len(order)] for spot, at in enumerate(order)}
    return lax.ppermute(value, "expert", [(2 * at + core, 2 * follow[at] + core) for at in order for core in range(2)])


def swap(value, n_expert):
    return lax.ppermute(value, "expert", [(at, at ^ 1) for at in range(n_expert)])


def flip(value, mask):
    return lax.ppermute(value, "dp", [(at, at ^ mask) for at in range(4)])


def add(*values):
    return sum(value.astype(F32) for value in values)


class Order:
    def __init__(self, start):
        self.last = start

    def point(self, *values):
        *values, self.last = lax.optimization_barrier((*values, self.last))
        return values

    def after(self, value):
        return lax.optimization_barrier((value, self.last))[0]


def dense_shards(tokens, cotangent, expert_ids, gate_fixed, w_gate, w_up, w_down):
    n_expert = lax.axis_size("expert")
    n, width = tokens.shape
    ff = w_gate.shape[2]
    half, cut = width // 2, width // 8

    def ring(value, name):
        with jax.named_scope(name):
            return step(order.after(value), n_expert)

    def twin(value, name):
        with jax.named_scope(name):
            return swap(order.after(value), n_expert)

    def flips(pair, masks, name):
        with jax.named_scope(name):
            return [flip(order.after(value), mask) for value, mask in zip(pair, masks)]

    def launch(name, kernel, outs, ins, scratch=(), smem=0, copies=0):
        return call(name, kernel, outs, [*ins[:smem], order.after(ins[smem]), *ins[smem + 1 :]], scratch, smem, copies)

    gate_w, up_w, down_w = w_gate[0].T, w_up[0].T, w_down[0]
    me = lax.axis_index("dp")
    offs = [((me ^ rel) * 2 + part) * (width // 8) for rel, part in PIECES]
    offs = jnp.stack([*offs, lax.axis_index("expert")]).astype(jnp.int32)

    def forward(slot, *parts):
        pair = 2 * n
        return launch(
            f"forward_{slot}",
            forward_kernel,
            [((pair, ff), BF16), ((pair, ff), F32), ((pair, ff), F32), ((pair, half), BF16), ((pair, half), BF16)],
            [offs, *parts, gate_w, up_w],
            [((pair, width), BF16)],
            smem=1,
        )

    def backward(slot, ahead, *parts):
        pair = 2 * n
        return launch(
            f"backward_{slot}",
            backward_kernel,
            [((n, width), BF16)] * 2 + [((pair, ff), BF16)] * 2 + [((pair, half), BF16)] * 2,
            [offs, *ahead[:3], down_w, *parts],
            [((pair, width + 128), BF16), ((pair, width), BF16)],
            smem=1,
        )

    def grads(name, groups, *lists):
        return launch(
            name,
            partial(grads_kernel, groups),
            [((len(groups), ff, half // 2), BF16)] * 2,
            [part for parts in lists for part in parts],
            [((8 * n, ff), BF16), ((8 * n, half), BF16)],
        )

    def row_grads(name, slot, cuts=1):
        return launch(
            name,
            rows_kernel,
            [((n, width), BF16)] + [((n // cuts, width), BF16)] * cuts,
            [d_gates[slot], d_ups[slot], gate_w, up_w],
        )

    def pick(value, which):
        return value[which * (n // 2) : (which + 1) * (n // 2)]

    def kept(mine, other, which=None):
        return add(mine, other) if which is None else add(pick(mine, which), pick(other, which))

    def total(near, last, at):
        return jnp.concatenate([add(part[at], more[at]) for part, more in zip(near, last)], axis=1)

    def whole(part_a, part_b, mine, other):
        return jnp.concatenate(
            [add(part_a, kept(mine, other, 0)), add(part_b, kept(mine, other, 1))], axis=0
        ).astype(BF16)

    def twins(value, name):
        return [twin(pick(value, at), f"{name}_{at}") for at in range(2)]

    def early(*parts):
        return launch(
            "early",
            early_kernel,
            [((1, ff, half // 2), BF16)] * 2 + [((2 * n, half), BF16), ((2 * n, 128), F32)],
            [offs, ahead, f3[0], *parts],
            [((2 * n, half + 128), BF16)],
            smem=1,
        )

    def outputs(name, hid, gates):
        return launch(name, out_kernel, [((n, width), BF16)] * 2, [hid, down_w, gates])

    def backward_last(gates, dy_s, *parts):
        return launch(
            "backward_3",
            last_kernel,
            [((2 * n, ff), BF16)] * 2 + [((2 * n, half), BF16)],
            [offs, gates, *f3[1:3], down_w, dy_s, *parts],
            [((2 * n, width), BF16)],
            smem=1,
        )

    def sums(name, *terms, rows=n, low=0):
        terms = [term if isinstance(term, list) else [term] for term in terms]
        spec = tuple((len(term), low if term[0].shape[0] > rows else 0) for term in terms)
        ins = [part for term in terms for part in term]
        return launch(name, partial(sum_kernel, spec), [((rows, width), BF16)], ins)[0]

    order = Order(jnp.zeros((8, 128), F32))
    t0 = tokens
    t1, p0 = ring(t0, "t1"), twin(t0, "p0")
    c0 = launch("pack", pack_kernel, [((n, width + 128), BF16)], [expert_ids, gate_fixed, cotangent])[0]
    c1, q0 = ring(c0, "c1"), twin(c0, "q0")
    (t1,) = order.point(t1)
    t2, p1 = ring(t1, "t2"), twin(t1, "p1")
    c1, p0, p1 = order.point(c1, p0, p1)
    c2, q1 = ring(c1, "c2"), twin(c1, "q1")
    f0 = forward(0, t0, p0)
    f1 = forward(1, t1, p1)
    t2, f0[0], f1[0] = order.point(t2, f0[0], f1[0])
    t3, p2 = ring(t2, "t3"), twin(t2, "p2")
    b0 = backward(0, f0, c0, q0)
    b1 = backward(1, f1, c1, q1)
    o1 = twin(b1[1], "o1")
    c2, p2, b0[0], b1[0] = order.point(c2, p2, b0[0], b1[0])
    c2s, c2k = launch("split", split_kernel, [((n, half + 128), BF16), ((n, half), BF16)], [offs, c2], smem=1)
    c3s = ring(c2s, "c3s")
    q2 = twins(c2, "q2")
    f2 = forward(2, t2, p2)
    b2 = backward(2, f2, c2, *q2)
    o2 = twin(b2[1], "o2")
    ahead = launch(
        "ahead",
        ahead_kernel,
        [((ff, half), F32)],
        [f0[0], f1[0], f2[0], b0[4], b1[4], b2[4]],
        [((6 * n, ff), BF16), ((6 * n, half), BF16)],
    )[0]
    t3, o1, ahead, f2[0], b2[0] = order.point(t3, o1, ahead, f2[0], b2[0])
    c3k = ring(c2k, "c3k")
    p3 = twins(t3, "p3")
    f3 = forward(3, t3, *p3)
    c3s, o2, *f3 = order.point(c3s, o2, *f3)
    m = ring(sums("add_m1", b1[0], o1), "m1")
    q3s = twins(c3s, "q3s")
    hids, facs_g, facs_u, rows_s, rows_k = ([f[at] for f in (f0, f1, f2, f3)] for at in range(5))
    *sent, dy3, gates3 = early(c3s, *q3s)
    dy3, *sent = order.point(dy3, *sent)
    down_came = flips(sent, (1, 2), "d1")
    out3 = outputs("out_3", f3[0], gates3)
    (c3k,) = order.point(c3k)
    q3k = twins(c3k, "q3k")
    b3 = backward_last(gates3, dy3, c3k, *q3k)
    b3 = [*out3, *b3[:2], dy3, b3[2]]
    outs_m, outs_o, d_gates, d_ups, dys_s, dys_k = ([b[at] for b in (b0, b1, b2, b3)] for at in range(6))
    sent = grads("both_s", ((0, 2), (1, 2)), d_gates, d_ups, rows_s)
    d_gates[1], *sent = order.point(d_gates[1], *sent)
    m1, r1 = row_grads("rows_1", 1)
    m, d_gates[2], r1 = order.point(m, d_gates[2], r1)
    m = ring(sums("add_m2", m, outs_m[2], o2), "m2")
    r1, o3 = twin(r1, "r1"), twin(outs_o[3], "o3")
    r1, o3, d_gates[0] = order.point(r1, o3, d_gates[0])
    m2, r2 = row_grads("rows_2", 2)
    r2, d_gates[0], *down_came = order.point(r2, d_gates[0], *down_came)
    both_came = flips(sent, (1, 2), "gu1")
    g = ring(sums("add_g1", m1, r1), "ga1")
    o0 = twin(outs_o[0], "o0")
    m3, r3 = row_grads("rows_3", 3)
    m0, r0 = row_grads("rows_0", 0)
    own = grads("kept_k", ((0, 2), (1, 2), (3, 4)), d_gates, d_ups, rows_k, hids, dys_k)
    m, o0, m3, r3, m0, r0, *own = order.point(m, o0, m3, r3, m0, r0, *own)
    m = ring(sums("add_m3", m, outs_m[3], o3), "m3")
    r2 = twin(r2, "r2")
    g, r2 = order.point(g, r2)
    g = ring(sums("add_g2", g, m2, r2), "ga2")
    r3 = twin(r3, "r3")
    both_came[0], both_came[1], m = order.point(*both_came, m)
    parts = [*both_came, *down_came, *own]
    far = launch("cross", partial(cross_kernel, False), [((3, ff, cut), BF16)] * 2, parts)
    far = order.point(*far)
    last = flips(far, (2, 1), "last")
    near_a, near_b = launch("settle", partial(cross_kernel, True), [((3, ff, cut), F32)] * 2, parts)
    g, r3 = order.point(g, r3)
    g = ring(add(g, kept(m3, r3)).astype(BF16), "ga3")
    r0 = twin(r0, "r0")
    mixed = sums("add_m0", m, outs_m[0], o0)
    g, r0, mixed, near_a, near_b = order.point(g, r0, mixed, near_a, near_b)
    token_grad = add(g, kept(m0, r0)).astype(BF16)
    token_grad, *last = order.point(token_grad, *last)
    grad_gate, grad_up, grad_down = launch(
        "finish",
        finish_kernel,
        [((ff, 2 * cut), F32)] * 3,
        [near_a, near_b, *last],
        [((3, ff, 2 * cut), F32)],
        copies=3,
    )
    return (mixed, token_grad, grad_gate.T[None], grad_up.T[None], grad_down[None])


def shards(tokens, cotangent, expert_ids, gate_fixed, w_gate, w_up, w_down):
    n_expert = lax.axis_size("expert")
    rows, width = tokens.shape
    capacity = 4 * rows * expert_ids.shape[1] // (3 * n_expert)
    dense = capacity >= rows and n_expert == 8 and lax.axis_size("dp") == 4 and rows == 128 and width % 2048 == 0
    run = dense_shards if dense else slot_shards
    return run(tokens, cotangent, expert_ids, gate_fixed, w_gate, w_up, w_down)


def solution(mesh):
    in_specs = (
        P(("dp", "expert"), None),
        P(("dp", "expert"), None),
        P(("dp", "expert"), None),
        P(("dp", "expert"), None),
        P("expert", None, None),
        P("expert", None, None),
        P("expert", None, None),
    )
    out_specs = (
        P(("dp", "expert"), None),
        P(("dp", "expert"), None),
        P("expert", "dp", None),
        P("expert", "dp", None),
        P("expert", None, "dp"),
    )
    return jax.shard_map(shards, mesh=mesh, in_specs=in_specs, out_specs=out_specs, check_vma=False)
```

```python
from functools import partial

import jax
import jax.numpy as jnp
from jax import lax
from jax.experimental import pallas as pl
from jax.experimental.pallas import tpu as pltpu
from jax.sharding import PartitionSpec as P


def contract(left, right):
    return lax.dot_general(
        left, right, (((0,), (0,)), ((), ())), preferred_element_type=jnp.float32
    )


def trans_dot(left, right):
    return lax.dot_general(
        left, right, (((1,), (1,)), ((), ())), preferred_element_type=jnp.float32
    )


def forward_rows(gate_w, up_w, down_w, rows_in):
    gate_pre = jnp.dot(rows_in, gate_w, preferred_element_type=jnp.float32)
    up_pre = jnp.dot(rows_in, up_w, preferred_element_type=jnp.float32)
    hidden = (gate_pre * jax.nn.sigmoid(gate_pre) * up_pre).astype(jnp.bfloat16)
    expert_out = jnp.dot(hidden, down_w, preferred_element_type=jnp.float32).astype(jnp.bfloat16)
    return (expert_out, gate_pre, up_pre, hidden)


def backward_rows(gate_w, up_w, down_w, dy_rows, gate_pre, up_pre):
    sigma = jax.nn.sigmoid(gate_pre)
    activ = gate_pre * sigma
    d_hidden = trans_dot(dy_rows, down_w)
    d_gate = (d_hidden * up_pre * (sigma * (1.0 + gate_pre * (1.0 - sigma)))).astype(jnp.bfloat16)
    d_up = (d_hidden * activ).astype(jnp.bfloat16)
    d_rows = (trans_dot(d_gate, gate_w) + trans_dot(d_up, up_w)).astype(jnp.bfloat16)
    return (d_rows, d_gate, d_up)


def slot_shards(tokens, cotangent, expert_ids, gate_fixed, w_gate, w_up, w_down):
    n_expert = lax.axis_size("expert")
    tok_rows = tokens.shape[0]
    width = tokens.shape[1]
    top_k = expert_ids.shape[1]
    capacity = 4 * tok_rows * top_k // (3 * n_expert)
    slot_count = n_expert * capacity
    gate_w = w_gate[0]
    up_w = w_up[0]
    down_w = w_down[0]
    flat_ids = expert_ids.reshape(-1)
    onehot = (flat_ids[:, None] == jnp.arange(n_expert, dtype=jnp.int32)[None, :]).astype(jnp.int32)
    before = jnp.cumsum(onehot, axis=0) - onehot
    rank_in = jnp.sum(before * onehot, axis=1)
    counts = jnp.sum(onehot, axis=0)
    slot_of = flat_ids * capacity + rank_in
    owner = jnp.arange(flat_ids.shape[0], dtype=jnp.int32) // top_k
    slot_token = jnp.zeros((slot_count,), jnp.int32).at[slot_of].set(owner)
    gate_values = gate_fixed.reshape(-1).astype(jnp.float32) / 65536.0
    slot_gate = jnp.zeros((slot_count,), jnp.float32).at[slot_of].set(gate_values)
    outgoing = jnp.where(
        (slot_gate > 0.0)[:, None], tokens[slot_token], jnp.zeros((), tokens.dtype)
    )
    received, arrived = (
        lax.all_to_all(outgoing, "expert", split_axis=0, concat_axis=0, tiled=True),
        lax.all_to_all(counts, "expert", split_axis=0, concat_axis=0, tiled=True),
    )

    def run_rows(row_fn, inputs):
        return row_fn(*inputs)

    def fold_rows(left, right):
        return contract(left, right)

    expert_out, gate_pre, up_pre, hidden = run_rows(
        partial(forward_rows, gate_w, up_w, down_w), (received,)
    )
    returned = lax.all_to_all(expert_out, "expert", split_axis=0, concat_axis=0, tiled=True)
    mixed_rows = returned[slot_of].astype(jnp.float32).reshape(tok_rows, top_k, width)
    mixed = jnp.sum(mixed_rows * gate_values.reshape(tok_rows, top_k)[:, :, None], axis=1).astype(
        jnp.bfloat16
    )
    dy_out = (cotangent[slot_token].astype(jnp.float32) * slot_gate[:, None]).astype(jnp.bfloat16)
    dy_in = lax.all_to_all(dy_out, "expert", split_axis=0, concat_axis=0, tiled=True)
    d_rows, d_gate, d_up = run_rows(
        partial(backward_rows, gate_w, up_w, down_w), (dy_in, gate_pre, up_pre)
    )
    back_rows = lax.all_to_all(d_rows, "expert", split_axis=0, concat_axis=0, tiled=True)
    token_grad = jnp.sum(
        back_rows[slot_of].astype(jnp.float32).reshape(tok_rows, top_k, width), axis=1
    ).astype(jnp.bfloat16)
    grad_gate, grad_up, grad_down = (
        lax.psum_scatter(
            fold_rows(received, d_gate).astype(jnp.bfloat16), "dp", scatter_dimension=0, tiled=True
        ).astype(jnp.float32),
        lax.psum_scatter(
            fold_rows(received, d_up).astype(jnp.bfloat16), "dp", scatter_dimension=0, tiled=True
        ).astype(jnp.float32),
        lax.psum_scatter(
            fold_rows(hidden, dy_in).astype(jnp.bfloat16), "dp", scatter_dimension=1, tiled=True
        ).astype(jnp.float32),
    )
    return (mixed, token_grad, grad_gate[None], grad_up[None], grad_down[None])


BF16, F32 = jnp.bfloat16, jnp.float32
VMEM = pl.BlockSpec(memory_space=pltpu.VMEM)
SMEM = pl.BlockSpec(memory_space=pltpu.SMEM)
PIECES = ((1, 0), (3, 0), (2, 1), (3, 1), (0, 0), (2, 0), (0, 1), (1, 1))


def tie(*values):
    return lax.optimization_barrier(values)


def nt(left, right):
    return lax.dot_general(left, right, (((1,), (1,)), ((), ())), preferred_element_type=F32)


def nn(left, right):
    return lax.dot_general(left, right, (((1,), (0,)), ((), ())), preferred_element_type=F32)


def tn(left, right):
    return lax.dot_general(left, right, (((0,), (0,)), ((), ())), preferred_element_type=F32)


def call(name, kernel, outs, ins, scratch=(), smem=0, flops=1):
    return list(pl.pallas_call(
        kernel,
        name=name,
        out_shape=[jax.ShapeDtypeStruct(shape, dtype) for shape, dtype in outs],
        in_specs=[SMEM] * smem + [VMEM] * (len(ins) - smem),
        out_specs=[VMEM] * len(outs),
        scratch_shapes=[pltpu.VMEM(shape, dtype) for shape, dtype in scratch],
        compiler_params=pltpu.CompilerParams(vmem_limit_bytes=16 * 1024 * 1024),
        cost_estimate=pl.CostEstimate(flops=flops, bytes_accessed=1, transcendentals=0),
    )(*ins))


def pack_kernel(ids, gates, cot, out):
    n, width = cot.shape
    column = lax.broadcasted_iota(jnp.int32, (n, 128), 1)
    extra = jnp.zeros((n, 128), jnp.int32)
    for at in range(ids.shape[1]):
        expert, gate = ids[:, at : at + 1], gates[:, at : at + 1]
        extra += jnp.where(column == expert, gate >> 8, 0)
        extra += jnp.where(column == expert + 8, gate & 255, 0)
    out[:, :width] = cot[...]
    out[:, width:] = extra.astype(F32).astype(BF16)


def gate_column(expert, extra):
    column = lax.broadcasted_iota(jnp.int32, extra.shape, 1)
    scale = jnp.where(column == expert, 256.0, jnp.where(column == expert + 8, 1.0, 0.0))
    return jnp.sum(extra.astype(F32) * scale, axis=1, keepdims=True) / 65536.0


def forward_kernel(offs, *refs):
    parts, (gate, up, hid, fac_g, fac_u, rows_s, rows_k, rows) = refs[:-8], refs[-8:]
    size = rows.shape[1] // 8
    stack(parts, rows)
    gate_pre = nt(rows[...], gate[...])
    up_pre = nt(rows[...], up[...])
    sigma = jax.nn.sigmoid(gate_pre)
    activ = gate_pre * sigma
    hid[...] = (activ * up_pre).astype(BF16)
    fac_g[...] = up_pre * (sigma * (1.0 + gate_pre * (1.0 - sigma)))
    fac_u[...] = activ
    for at in range(8):
        here = pl.ds(pl.multiple_of(offs[at], size), size)
        (rows_s if at < 4 else rows_k)[:, pl.ds(at % 4 * size, size)] = rows[:, here]


def stack(parts, whole):
    at = 0
    for part in parts:
        whole[at : at + part.shape[0], :] = part[...]
        at += part.shape[0]


def backward_kernel(offs, hid, fac_g, fac_u, down, *refs):
    parts, (out_m, out_o, d_gate, d_up, dy_s, dy_k, held, dy) = refs[:-8], refs[-8:]
    n, width = out_m.shape
    size = width // 8
    stack(parts, held)
    out = nn(hid[...], down[...])
    for at, result in enumerate((out_m, out_o)):
        part = slice(at * n, (at + 1) * n)
        gate = gate_column(offs[8], held[part, width:])
        dy[part, :] = (held[part, :width].astype(F32) * gate).astype(BF16)
        result[...] = (out[part] * gate).astype(BF16)
    d_hid = nt(dy[...], down[...])
    d_gate[...] = (d_hid * fac_g[...]).astype(BF16)
    d_up[...] = (d_hid * fac_u[...]).astype(BF16)
    for at in range(8):
        here = pl.ds(pl.multiple_of(offs[at], size), size)
        (dy_s if at < 4 else dy_k)[:, pl.ds(at % 4 * size, size)] = dy[:, here]


def split_kernel(offs, whole, part_s, part_k):
    width = 2 * part_k.shape[1]
    size = width // 8
    for at in range(8):
        here = pl.ds(pl.multiple_of(offs[at], size), size)
        (part_s if at < 4 else part_k)[:, pl.ds(at % 4 * size, size)] = whole[:, here]
    part_s[:, width // 2 :] = whole[:, width:]


def ahead_kernel(*refs):
    hids, dys, (total, left, right) = refs[:3], refs[3:6], refs[6:]
    stack(hids, left)
    stack(dys, right)
    total[...] = tn(left[...], right[...])


def early_kernel(offs, ahead, hid, *refs):
    parts, (out_a, out_b, dy, gates, held) = refs[:-5], refs[-5:]
    stack(parts, held)
    half = dy.shape[1]
    gate = gate_column(offs[8], held[:, half:])
    gates[...] = jnp.broadcast_to(gate, gates.shape)
    dy[...] = (held[:, :half].astype(F32) * gate).astype(BF16)
    out_a[0, :, :] = (ahead[:, : half // 2] + tn(hid[...], dy[:, : half // 2])).astype(BF16)
    out_b[0, :, :] = (ahead[:, half // 2 :] + tn(hid[...], dy[:, half // 2 :])).astype(BF16)


def out_kernel(hid, down, gates, out_m, out_o):
    n = out_m.shape[0]
    out = nn(hid[...], down[...]) * gates[:, :1]
    out_m[...] = out[:n].astype(BF16)
    out_o[...] = out[n:].astype(BF16)


def sum_kernel(spec, *refs):
    *parts, out = refs
    total, at = 0.0, 0
    for count, low in spec:
        if count == 1:
            term = parts[at][low : low + out.shape[0], :]
        else:
            term = jnp.concatenate([part[...] for part in parts[at : at + count]], axis=0)
        total = total + term.astype(F32)
        at += count
    out[...] = total.astype(BF16)


def last_kernel(offs, gates, fac_g, fac_u, down, dy_s, *refs):
    parts, (d_gate, d_up, dy_k, dy) = refs[:-4], refs[-4:]
    size = down.shape[1] // 8
    stack(parts, dy_k)
    dy_k[...] = (dy_k[...].astype(F32) * gates[:, :1]).astype(BF16)
    for at in range(8):
        here = pl.ds(pl.multiple_of(offs[at], size), size)
        dy[:, here] = (dy_s if at < 4 else dy_k)[:, pl.ds(at % 4 * size, size)]
    d_hid = nt(dy[...], down[...])
    d_gate[...] = (d_hid * fac_g[...]).astype(BF16)
    d_up[...] = (d_hid * fac_u[...]).astype(BF16)


def grads_kernel(groups, *refs):
    ins, (out_a, out_b, left, right) = refs[:-4], refs[-4:]
    half = right.shape[1] // 2
    held = None
    for at, (first, second) in enumerate(groups):
        stack(ins[4 * first : 4 * first + 4], left)
        if second != held:
            stack(ins[4 * second : 4 * second + 4], right)
            held = second
        out_a[at, :, :] = tn(left[...], right[:, :half]).astype(BF16)
        out_b[at, :, :] = tn(left[...], right[:, half:]).astype(BF16)


def cross_kernel(near, came, down, own, out):
    cut = out.shape[2]
    part = slice(0, cut) if near else slice(cut, 2 * cut)
    for at in range(3):
        first = down[0, :, part] if at == 2 else came[at, :, part]
        out[at, :, :] = (first.astype(F32) + own[at, :, part].astype(F32)).astype(out.dtype)


def finish_kernel(near_a, near_b, last_a, last_b, *outs):
    cut = near_a.shape[2]
    for at, out in enumerate(outs):
        out[:, :cut] = near_a[at, :, :] + last_a[at, :, :].astype(F32)
        out[:, cut:] = near_b[at, :, :] + last_b[at, :, :].astype(F32)


def rows_kernel(*refs):
    d_gate, d_up, gate, up, mine, *others = refs
    n = mine.shape[0]
    size = others[0].shape[0]
    both = nn(d_gate[...], gate[...]) + nn(d_up[...], up[...])
    mine[...] = both[:n].astype(BF16)
    for at, other in enumerate(others):
        other[...] = both[n + at * size : n + (at + 1) * size].astype(BF16)


def ring_order(count):
    return [0] + list(range(1, count, 2)) + [at for at in range(count - 1, 1, -1) if at % 2 == 0]


def step(value, n_expert):
    order = ring_order(n_expert // 2)
    follow = {at: order[(spot + 1) % len(order)] for spot, at in enumerate(order)}
    return lax.ppermute(value, "expert", [(2 * at + core, 2 * follow[at] + core) for at in order for core in range(2)])


def swap(value, n_expert):
    return lax.ppermute(value, "expert", [(at, at ^ 1) for at in range(n_expert)])


def flip(value, mask):
    return lax.ppermute(value, "dp", [(at, at ^ mask) for at in range(4)])


def add(*values):
    return sum(value.astype(F32) for value in values)


class Order:
    def __init__(self, start):
        self.last = start

    def point(self, *values):
        *values, self.last = lax.optimization_barrier((*values, self.last))
        return values

    def after(self, value):
        return lax.optimization_barrier((value, self.last))[0]


def dense_shards(tokens, cotangent, expert_ids, gate_fixed, w_gate, w_up, w_down):
    n_expert = lax.axis_size("expert")
    n, width = tokens.shape
    ff = w_gate.shape[2]
    half, cut = width // 2, width // 8

    def ring(value, name):
        with jax.named_scope(name):
            return step(order.after(value), n_expert)

    def twin(value, name):
        with jax.named_scope(name):
            return swap(order.after(value), n_expert)

    def flips(pair, masks, name):
        with jax.named_scope(name):
            return [flip(order.after(value), mask) for value, mask in zip(pair, masks)]

    def launch(name, kernel, outs, ins, scratch=(), smem=0, flops=1):
        return call(name, kernel, outs, [*ins[:smem], order.after(ins[smem]), *ins[smem + 1 :]], scratch, smem, flops)

    gate_w, up_w, down_w = w_gate[0].T, w_up[0].T, w_down[0]
    me = lax.axis_index("dp")
    offs = [((me ^ rel) * 2 + part) * (width // 8) for rel, part in PIECES]
    offs = jnp.stack([*offs, lax.axis_index("expert")]).astype(jnp.int32)

    def forward(slot, *parts):
        pair = 2 * n
        return launch(
            f"forward_{slot}",
            forward_kernel,
            [((pair, ff), BF16), ((pair, ff), F32), ((pair, ff), F32), ((pair, half), BF16), ((pair, half), BF16)],
            [offs, *parts, gate_w, up_w],
            [((pair, width), BF16)],
            smem=1,
        )

    def backward(slot, ahead, *parts):
        pair = 2 * n
        return launch(
            f"backward_{slot}",
            backward_kernel,
            [((n, width), BF16)] * 2 + [((pair, ff), BF16)] * 2 + [((pair, half), BF16)] * 2,
            [offs, *ahead[:3], down_w, *parts],
            [((pair, width + 128), BF16), ((pair, width), BF16)],
            smem=1,
        )

    def grads(name, groups, *lists):
        return launch(
            name,
            partial(grads_kernel, groups),
            [((len(groups), ff, half // 2), BF16)] * 2,
            [part for parts in lists for part in parts],
            [((8 * n, ff), BF16), ((8 * n, half), BF16)],
        )

    def row_grads(name, slot, cuts=1):
        return launch(
            name,
            rows_kernel,
            [((n, width), BF16)] + [((n // cuts, width), BF16)] * cuts,
            [d_gates[slot], d_ups[slot], gate_w, up_w],
        )

    def pick(value, which):
        return value[which * (n // 2) : (which + 1) * (n // 2)]

    def kept(mine, other, which=None):
        return add(mine, other) if which is None else add(pick(mine, which), pick(other, which))

    def total(near, last, at):
        return jnp.concatenate([add(part[at], more[at]) for part, more in zip(near, last)], axis=1)

    def whole(part_a, part_b, mine, other):
        return jnp.concatenate(
            [add(part_a, kept(mine, other, 0)), add(part_b, kept(mine, other, 1))], axis=0
        ).astype(BF16)

    def twins(value, name):
        return [twin(pick(value, at), f"{name}_{at}") for at in range(2)]

    def early(*parts):
        return launch(
            "early",
            early_kernel,
            [((1, ff, half // 2), BF16)] * 2 + [((2 * n, half), BF16), ((2 * n, 128), F32)],
            [offs, ahead, f3[0], *parts],
            [((2 * n, half + 128), BF16)],
            smem=1,
        )

    def outputs(name, hid, gates):
        return launch(name, out_kernel, [((n, width), BF16)] * 2, [hid, down_w, gates])

    def backward_last(gates, dy_s, *parts):
        return launch(
            "backward_3",
            last_kernel,
            [((2 * n, ff), BF16)] * 2 + [((2 * n, half), BF16)],
            [offs, gates, *f3[1:3], down_w, dy_s, *parts],
            [((2 * n, width), BF16)],
            smem=1,
        )

    def sums(name, *terms, rows=n, low=0):
        terms = [term if isinstance(term, list) else [term] for term in terms]
        spec = tuple((len(term), low if term[0].shape[0] > rows else 0) for term in terms)
        ins = [part for term in terms for part in term]
        return launch(name, partial(sum_kernel, spec), [((rows, width), BF16)], ins)[0]

    order = Order(jnp.zeros((8, 128), F32))
    t0 = tokens
    t1, p0 = ring(t0, "t1"), twin(t0, "p0")
    c0 = launch("pack", pack_kernel, [((n, width + 128), BF16)], [expert_ids, gate_fixed, cotangent])[0]
    c1, q0 = ring(c0, "c1"), twin(c0, "q0")
    (t1,) = order.point(t1)
    t2, p1 = ring(t1, "t2"), twin(t1, "p1")
    c1, p0, p1 = order.point(c1, p0, p1)
    c2, q1 = ring(c1, "c2"), twin(c1, "q1")
    f0 = forward(0, t0, p0)
    f1 = forward(1, t1, p1)
    t2, f0[0], f1[0] = order.point(t2, f0[0], f1[0])
    t3, p2 = ring(t2, "t3"), twin(t2, "p2")
    b0 = backward(0, f0, c0, q0)
    b1 = backward(1, f1, c1, q1)
    o1 = twin(b1[1], "o1")
    c2, p2, b0[0], b1[0] = order.point(c2, p2, b0[0], b1[0])
    c2s, c2k = launch("split", split_kernel, [((n, half + 128), BF16), ((n, half), BF16)], [offs, c2], smem=1)
    c3s = ring(c2s, "c3s")
    q2 = twins(c2, "q2")
    f2 = forward(2, t2, p2)
    b2 = backward(2, f2, c2, *q2)
    o2 = twin(b2[1], "o2")
    ahead = launch(
        "ahead",
        ahead_kernel,
        [((ff, half), F32)],
        [f0[0], f1[0], f2[0], b0[4], b1[4], b2[4]],
        [((6 * n, ff), BF16), ((6 * n, half), BF16)],
    )[0]
    t3, o1, ahead, f2[0], b2[0] = order.point(t3, o1, ahead, f2[0], b2[0])
    c3k = ring(c2k, "c3k")
    p3 = twins(t3, "p3")
    f3 = forward(3, t3, *p3)
    c3s, o2, *f3 = order.point(c3s, o2, *f3)
    m = ring(sums("add_m1", b1[0], o1), "m1")
    q3s = twins(c3s, "q3s")
    hids, facs_g, facs_u, rows_s, rows_k = ([f[at] for f in (f0, f1, f2, f3)] for at in range(5))
    *sent, dy3, gates3 = early(c3s, *q3s)
    dy3, *sent = order.point(dy3, *sent)
    down_came = flips(sent, (1, 2), "d1")
    out3 = outputs("out_3", f3[0], gates3)
    (c3k,) = order.point(c3k)
    q3k = twins(c3k, "q3k")
    b3 = backward_last(gates3, dy3, c3k, *q3k)
    b3 = [*out3, *b3[:2], dy3, b3[2]]
    outs_m, outs_o, d_gates, d_ups, dys_s, dys_k = ([b[at] for b in (b0, b1, b2, b3)] for at in range(6))
    sent = grads("both_s", ((0, 2), (1, 2)), d_gates, d_ups, rows_s)
    d_gates[1], *sent = order.point(d_gates[1], *sent)
    m1, r1 = row_grads("rows_1", 1)
    m, d_gates[2], r1 = order.point(m, d_gates[2], r1)
    m = ring(sums("add_m2", m, outs_m[2], o2), "m2")
    r1, o3 = twin(r1, "r1"), twin(outs_o[3], "o3")
    r1, o3, d_gates[0] = order.point(r1, o3, d_gates[0])
    m2, r2 = row_grads("rows_2", 2)
    r2, d_gates[0], *down_came = order.point(r2, d_gates[0], *down_came)
    both_came = flips(sent, (1, 2), "gu1")
    g = ring(sums("add_g1", m1, r1), "ga1")
    o0 = twin(outs_o[0], "o0")
    m3, r3 = row_grads("rows_3", 3)
    m0, r0 = row_grads("rows_0", 0)
    own = grads("kept_k", ((0, 2), (1, 2), (3, 4)), d_gates, d_ups, rows_k, hids, dys_k)
    m, o0, m3, r3, m0, r0, *own = order.point(m, o0, m3, r3, m0, r0, *own)
    m = ring(sums("add_m3", m, outs_m[3], o3), "m3")
    r2 = twin(r2, "r2")
    g, r2 = order.point(g, r2)
    g = ring(sums("add_g2", g, m2, r2), "ga2")
    r3 = twin(r3, "r3")
    last = [None, None]
    for at, mask in ((1, 1), (0, 2)):
        both_came[at], m = order.point(both_came[at], m)
        far = launch(
            f"cross_{at}",
            partial(cross_kernel, False),
            [((3, ff, cut), BF16)],
            [both_came[at], down_came[at], own[at]],
        )
        last[at] = flips(far, (mask,), "last")[0]
    near_a, near_b = (
        launch(
            f"settle_{at}",
            partial(cross_kernel, True),
            [((3, ff, cut), F32)],
            [both_came[at], down_came[at], own[at]],
        )[0]
        for at in range(2)
    )
    g, r3 = order.point(g, r3)
    g = ring(add(g, kept(m3, r3)).astype(BF16), "ga3")
    r0 = twin(r0, "r0")
    mixed = sums("add_m0", m, outs_m[0], o0)
    g, r0, mixed, near_a, near_b = order.point(g, r0, mixed, near_a, near_b)
    token_grad = add(g, kept(m0, r0)).astype(BF16)
    token_grad, *last = order.point(token_grad, *last)
    grad_gate, grad_up, grad_down = launch(
        "finish", finish_kernel, [((ff, 2 * cut), F32)] * 3, [near_a, near_b, *last]
    )
    return (mixed, token_grad, grad_gate.T[None], grad_up.T[None], grad_down[None])


def shards(tokens, cotangent, expert_ids, gate_fixed, w_gate, w_up, w_down):
    n_expert = lax.axis_size("expert")
    rows, width = tokens.shape
    capacity = 4 * rows * expert_ids.shape[1] // (3 * n_expert)
    dense = capacity >= rows and n_expert == 8 and lax.axis_size("dp") == 4 and rows == 128 and width % 2048 == 0
    run = dense_shards if dense else slot_shards
    return run(tokens, cotangent, expert_ids, gate_fixed, w_gate, w_up, w_down)


def solution(mesh):
    in_specs = (
        P(("dp", "expert"), None),
        P(("dp", "expert"), None),
        P(("dp", "expert"), None),
        P(("dp", "expert"), None),
        P("expert", None, None),
        P("expert", None, None),
        P("expert", None, None),
    )
    out_specs = (
        P(("dp", "expert"), None),
        P(("dp", "expert"), None),
        P("expert", "dp", None),
        P("expert", "dp", None),
        P("expert", None, "dp"),
    )
    return jax.shard_map(shards, mesh=mesh, in_specs=in_specs, out_specs=out_specs, check_vma=False)
```
